256 devices in a mesh: leaf: 32 (over z, y), head: 8 (over x, core).
Axes of the slice: x: 4, y: 4, z: 8, core: 2. Of those that a mesh axis runs over, the one named last changes fastest.
Arguments:
- hidden_states: bfloat16 [8192, 4096], P('leaf', 'head'), may hold values from -6 to 6
- upper_gradient: bfloat16 [8192, 4096], P('leaf', 'head'), may hold values from -96 to 96
- w_query: bfloat16 [4096, 4096], P(None, 'head'), may hold values from -0.09375 to 0.09375
- key_projection: bfloat16 [4096, 1024], P(None, 'head'), may hold values from -0.09375 to 0.09375
- value_projection: bfloat16 [4096, 1024], P(None, 'head'), may hold values from -0.09375 to 0.09375
- query_gain: float32 [128], replicated, may hold values from 0.5 to 1.5
- key_norm_gain: float32 [128], replicated, may hold values from 0.5 to 1.5
- readout: bfloat16 [4096], P('head'), may hold values from -6 to 6
- cached_prefix_keys: bfloat16 [32, 1024, 1024], P(None, 'leaf', 'head'), may hold values from -6 to 6
- cached_prefix_values: bfloat16 [32, 1024, 1024], P(None, 'leaf', 'head'), may hold values from -6 to 6
- prefix_lengths: int32 [32], replicated, may hold values from 128 to 1024, as said below
- parents: int32 [32], P('leaf'), may hold values from 0 to 31
- visits: int32 [32], P('leaf'), may hold values from 1 to 64
Outputs:
- grad_hidden: bfloat16 [8192, 4096], P('leaf', 'head')
- grad_prefix_keys: bfloat16 [32, 1024, 1024], P(None, 'leaf', 'head')
- grad_prefix_values: bfloat16 [32, 1024, 1024], P(None, 'leaf', 'head')
The draws below stay inside these ranges and needn't reach their ends.
Inputs may be any that keep to these rules, and one draw needn't show every extreme that they name: Node n's prefix occupies its first prefix_lengths[n] rows; some node uses all 1024 rows.
All inputs are finite; a program needn't handle non-finite values.
Results may differ from the reference program's by a relative error of at most 0.02.
Values may be sent and summed in bfloat16 or wider, within the bound.
A program may use at most 192 MiB of HBM per device.

```python
import jax
import jax.numpy as jnp
from jax import lax

MODEL_WIDTH = 4096
QUERY_HEADS = 32
KEY_VALUE_HEADS = 8
HEAD_SIZE = 128
STEP_TOKENS = 256
STEPS = 32
TREE_NODES = 32
PREFIX_ROWS = 1024
TOKENS = 8192
N_HEAD = 8


def draw_prefix_lengths(key, part):
    key = jax.random.fold_in(key, 11)
    first, second = jax.random.split(key)
    values = jax.random.randint(first, (TREE_NODES,), PREFIX_ROWS // 8, PREFIX_ROWS + 1)
    longest = jax.random.randint(second, (), 0, TREE_NODES)
    return jnp.where(jnp.arange(TREE_NODES) == longest, PREFIX_ROWS, values).astype(jnp.int32)


def place_ends(entries, own_key, low, high):
    longest = entries.shape.index(max(entries.shape))
    spots = []
    for shift in (0, 1):
        where = [jax.random.randint(jax.random.fold_in(own_key, axis), (), 0, length) for axis, length in enumerate(entries.shape)]
        where[longest] = (where[longest] + shift) % entries.shape[longest]
        spots.append(tuple(where))
    return entries.at[spots[0]].set(low).at[spots[1]].set(high)


def block_scale(rng, shape, cuts, least, high):
    level, own = 1.0, jax.random.fold_in(rng, 6)
    for dim, blocks in cuts:
        draws = jnp.exp(jax.random.uniform(jax.random.fold_in(own, dim), (blocks,), jnp.float32, least / len(cuts), high / len(cuts)))
        level = level * jnp.repeat(draws, shape[dim] // blocks).reshape([-1 if axis == dim else 1 for axis in range(len(shape))])
    return level


def gaussian(stream_key, shape, scale, reach, pieces=(), kind=jnp.bfloat16):
    values = jax.random.normal(stream_key, shape, jnp.float32) * scale
    if len(pieces) > 0:
        values = block_scale(stream_key, shape, pieces, -0.22, 0.18) * values
    return jnp.clip(values, min=-reach, max=reach).astype(kind)


def setup_inputs(seed: int = 0) -> dict:
    arg_keys = jax.random.split(jax.random.key(seed), 14)
    return {
        "hidden_states": gaussian(arg_keys[0], (TOKENS, MODEL_WIDTH), 1.0, 6.0, ((0, 32), (1, 8))),
        "upper_gradient": gaussian(arg_keys[1], (TOKENS, QUERY_HEADS * HEAD_SIZE), 16.0, 96.0, ((0, 32), (1, 8))),
        "w_query": gaussian(arg_keys[2], (MODEL_WIDTH, QUERY_HEADS * HEAD_SIZE), MODEL_WIDTH ** -0.5, 0.09375, ((1, 8),)),
        "key_projection": gaussian(arg_keys[3], (MODEL_WIDTH, KEY_VALUE_HEADS * HEAD_SIZE), MODEL_WIDTH ** -0.5, 0.09375, ((1, 8),)),
        "value_projection": gaussian(arg_keys[4], (MODEL_WIDTH, KEY_VALUE_HEADS * HEAD_SIZE), MODEL_WIDTH ** -0.5, 0.09375, ((1, 8),)),
        "query_gain": jnp.clip(1.0 + 0.1 * jax.random.normal(arg_keys[5], (HEAD_SIZE,), jnp.float32), 0.5, 1.5),
        "key_norm_gain": jnp.clip(1.0 + 0.1 * jax.random.normal(arg_keys[6], (HEAD_SIZE,), jnp.float32), 0.5, 1.5),
        "readout": gaussian(arg_keys[7], (QUERY_HEADS * HEAD_SIZE,), 1.0, 6.0, ((0, 8),)),
        "cached_prefix_keys": gaussian(arg_keys[8], (TREE_NODES, PREFIX_ROWS, KEY_VALUE_HEADS * HEAD_SIZE), 1.0, 6.0, ((1, 32), (2, 8))),
        "cached_prefix_values": gaussian(arg_keys[9], (TREE_NODES, PREFIX_ROWS, KEY_VALUE_HEADS * HEAD_SIZE), 1.0, 6.0, ((1, 32), (2, 8))),
        "prefix_lengths": draw_prefix_lengths(jax.random.fold_in(arg_keys[13], 71), 0),
        "parents": place_ends(jax.random.randint(arg_keys[11], (STEPS,), 0, TREE_NODES), jax.random.fold_in(arg_keys[11], 1), 0, TREE_NODES - 1).astype(jnp.int32),
        "visits": place_ends(jax.random.randint(arg_keys[12], (STEPS,), 1, 65), jax.random.fold_in(arg_keys[12], 1), 1, 64).astype(jnp.int32),
    }


EPS = 1e-06
ROPE_BASE = 1000000.0
LOSS_SCALE = 8192.0

def cast_lower_width(value):
    return lax.optimization_barrier(value.astype(jnp.bfloat16))

def rope_tables(positions, width):
    half = width // 2
    freq = ROPE_BASE ** (-2.0 * jnp.arange(half).astype(jnp.float32) / width)
    angle = positions.astype(jnp.float32)[:, None] * freq[None, :]
    return (jnp.cos(angle)[:, None, :], jnp.sin(angle)[:, None, :])

def apply_rotary(value, cosine_table, sine_table):
    half = value.shape[-1] // 2
    first, second = (value[..., :half], value[..., half:])
    return jnp.concatenate([first * cosine_table - second * sine_table, second * cosine_table + first * sine_table], -1)

def inverse_rotary(grad, cosine_table, sine_table):
    half = grad.shape[-1] // 2
    first, second = (grad[..., :half], grad[..., half:])
    return jnp.concatenate([first * cosine_table + second * sine_table, second * cosine_table - first * sine_table], -1)

def norm_forward(value, gain):
    inverse = lax.rsqrt(lax.optimization_barrier(jnp.mean(value * value, axis=-1, keepdims=True)) + EPS)
    return (value * inverse * gain, inverse)

def norm_reverse_pass(value, inverse, gain, grad):
    scaled = grad * gain
    return inverse * scaled - value * inverse ** 3 * lax.optimization_barrier(jnp.mean(value * scaled, axis=-1, keepdims=True))

def key_mask(length, prefix_len, step_len):
    keys_at = jnp.arange(prefix_len + step_len, dtype=jnp.int32)[None, :]
    rows_at = jnp.arange(step_len, dtype=jnp.int32)[:, None]
    inside = jnp.where(keys_at < prefix_len, keys_at < length, keys_at - prefix_len <= rows_at)
    return inside.astype(jnp.float32)

def forward_step(index, hidden_states, w_query, key_projection, value_projection, query_gain, key_norm_gain, readout, cached_prefix_keys, cached_prefix_values, prefix_lengths, parents):
    heads_per_group = QUERY_HEADS // KEY_VALUE_HEADS
    scale = HEAD_SIZE ** (-0.5)
    start_offset = (index * STEP_TOKENS).astype(jnp.int32)
    token_rows = lax.dynamic_slice_in_dim(hidden_states, start_offset, STEP_TOKENS, 0)
    parent_node = parents[index]
    length = prefix_lengths[parent_node]
    raw_query = jnp.dot(token_rows, w_query, preferred_element_type=jnp.float32).reshape(STEP_TOKENS, QUERY_HEADS, HEAD_SIZE)
    unnormed_key = jnp.dot(token_rows, key_projection, preferred_element_type=jnp.float32).reshape(STEP_TOKENS, KEY_VALUE_HEADS, HEAD_SIZE)
    sibling_values = cast_lower_width(jnp.dot(token_rows, value_projection, preferred_element_type=jnp.float32)).reshape(STEP_TOKENS, KEY_VALUE_HEADS, HEAD_SIZE)
    cosine_table, sine_table = rope_tables(length + jnp.arange(STEP_TOKENS, dtype=jnp.int32), HEAD_SIZE)
    normalized_query, inverse_q = norm_forward(raw_query, query_gain)
    normed_k, inverse_key_norm = norm_forward(unnormed_key, key_norm_gain)
    query_rows = cast_lower_width(apply_rotary(normalized_query, cosine_table, sine_table)).reshape(STEP_TOKENS, KEY_VALUE_HEADS, heads_per_group, HEAD_SIZE)
    sibling_keys = cast_lower_width(apply_rotary(normed_k, cosine_table, sine_table))
    joined_keys = jnp.concatenate([cached_prefix_keys[parent_node].reshape(PREFIX_ROWS, KEY_VALUE_HEADS, HEAD_SIZE), sibling_keys], 0)
    joined_values = jnp.concatenate([cached_prefix_values[parent_node].reshape(PREFIX_ROWS, KEY_VALUE_HEADS, HEAD_SIZE), sibling_values], 0)
    mask = key_mask(length, PREFIX_ROWS, STEP_TOKENS)
    logits = jnp.einsum('tkgd,jkd->kgtj', query_rows.astype(jnp.float32), joined_keys.astype(jnp.float32)) * scale
    weighted = jnp.exp(logits) * mask
    probs = weighted / lax.optimization_barrier(jnp.sum(weighted, axis=-1, keepdims=True))
    probs_low = cast_lower_width(probs)
    attended = jnp.einsum('kgtj,jkd->kgtd', probs_low.astype(jnp.float32), joined_values.astype(jnp.float32))
    gather_heads = readout.astype(jnp.float32).reshape(KEY_VALUE_HEADS, heads_per_group, HEAD_SIZE)
    score = jnp.sum(attended * gather_heads[:, :, None, :]) / STEP_TOKENS
    saved = (cosine_table, sine_table, raw_query, inverse_q, unnormed_key, inverse_key_norm, query_rows, joined_keys, joined_values, probs, probs_low, attended, gather_heads, parent_node, start_offset)
    return (score, saved)

def reference(hidden_states, upper_gradient, w_query, key_projection, value_projection, query_gain, key_norm_gain, readout, cached_prefix_keys, cached_prefix_values, prefix_lengths, parents, visits):
    heads_per_group = QUERY_HEADS // KEY_VALUE_HEADS
    scale = HEAD_SIZE ** (-0.5)
    operands = (hidden_states, w_query, key_projection, value_projection, query_gain, key_norm_gain, readout, cached_prefix_keys, cached_prefix_values, prefix_lengths, parents)

    def score_only(index):
        return forward_step(index, *operands)[0]
    scores = lax.map(score_only, jnp.arange(STEPS, dtype=jnp.int32))
    node_ids = jnp.arange(TREE_NODES, dtype=jnp.int32)
    onehot = (parents[None, :] == node_ids[:, None]).astype(jnp.float32)
    exp_scores = jnp.exp(scores)
    node_totals = lax.optimization_barrier(jnp.sum(onehot * exp_scores[None, :], axis=1))
    visit_totals = lax.optimization_barrier(jnp.sum(onehot * visits.astype(jnp.float32)[None, :], axis=1))
    sibling_probs = exp_scores / node_totals[parents]
    grad_scores = sibling_probs - visits.astype(jnp.float32) / visit_totals[parents]
    weights32 = (w_query.astype(jnp.float32).reshape(MODEL_WIDTH, N_HEAD, -1), key_projection.astype(jnp.float32).reshape(MODEL_WIDTH, N_HEAD, -1), value_projection.astype(jnp.float32).reshape(MODEL_WIDTH, N_HEAD, -1))

    def backward_step(carry, index):
        key_lookup, value_lookup = carry
        score, saved = forward_step(index, *operands)
        cosine_table, sine_table, raw_query, inverse_q, unnormed_key, inverse_key_norm, query_rows, joined_keys, joined_values, probs, probs_low, attended, gather_heads, parent_node, start_offset = saved
        upper_layers = lax.dynamic_slice_in_dim(upper_gradient, start_offset, STEP_TOKENS, 0).reshape(STEP_TOKENS, KEY_VALUE_HEADS, heads_per_group, HEAD_SIZE).transpose(1, 2, 0, 3).astype(jnp.float32)
        grad_out = upper_layers + LOSS_SCALE * grad_scores[index] / STEP_TOKENS * gather_heads[:, :, None, :]
        grad_low = cast_lower_width(grad_out)
        grad_probs = jnp.einsum('kgtd,jkd->kgtj', grad_low.astype(jnp.float32), joined_values.astype(jnp.float32))
        delta = lax.optimization_barrier(jnp.sum(grad_out * attended, axis=-1, keepdims=True))
        grad_logits = cast_lower_width(probs * (grad_probs - delta) * scale).astype(jnp.float32)
        grad_query = jnp.einsum('kgtj,jkd->tkgd', grad_logits, joined_keys.astype(jnp.float32)).reshape(STEP_TOKENS, QUERY_HEADS, HEAD_SIZE)
        full_key_gradient = jnp.einsum('kgtj,tkgd->jkd', grad_logits, query_rows.astype(jnp.float32))
        full_value_gradient = jnp.einsum('kgtj,kgtd->jkd', probs_low.astype(jnp.float32), grad_low.astype(jnp.float32))
        key_lookup = key_lookup.at[parent_node].add(full_key_gradient[:PREFIX_ROWS].reshape(PREFIX_ROWS, KEY_VALUE_HEADS * HEAD_SIZE))
        value_lookup = value_lookup.at[parent_node].add(full_value_gradient[:PREFIX_ROWS].reshape(PREFIX_ROWS, KEY_VALUE_HEADS * HEAD_SIZE))
        grad_rq = cast_lower_width(norm_reverse_pass(raw_query, inverse_q, query_gain, inverse_rotary(grad_query, cosine_table, sine_table))).reshape(STEP_TOKENS, QUERY_HEADS * HEAD_SIZE)
        rotated_key_gradient = cast_lower_width(norm_reverse_pass(unnormed_key, inverse_key_norm, key_norm_gain, inverse_rotary(full_key_gradient[PREFIX_ROWS:], cosine_table, sine_table))).reshape(STEP_TOKENS, KEY_VALUE_HEADS * HEAD_SIZE)
        value_row_gradient = cast_lower_width(full_value_gradient[PREFIX_ROWS:]).reshape(STEP_TOKENS, KEY_VALUE_HEADS * HEAD_SIZE)
        terms = None
        for grads, weight in ((grad_rq, weights32[0]), (rotated_key_gradient, weights32[1]), (value_row_gradient, weights32[2])):
            part = jnp.einsum('tgc,dgc->gtd', grads.astype(jnp.float32).reshape(STEP_TOKENS, N_HEAD, -1), weight)
            terms = part if terms is None else terms + part
        rounded = cast_lower_width(terms).astype(jnp.float32)
        grad_rows = lax.optimization_barrier(jnp.sum(rounded, axis=0)).astype(jnp.bfloat16)
        return ((key_lookup, value_lookup), grad_rows)
    offset_rotary_tables = (jnp.zeros((TREE_NODES, PREFIX_ROWS, KEY_VALUE_HEADS * HEAD_SIZE), jnp.float32), jnp.zeros((TREE_NODES, PREFIX_ROWS, KEY_VALUE_HEADS * HEAD_SIZE), jnp.float32))
    tables, grad_rows = lax.scan(backward_step, offset_rotary_tables, jnp.arange(STEPS, dtype=jnp.int32))
    grad_hidden = grad_rows.reshape(TOKENS, MODEL_WIDTH)
    return (grad_hidden, tables[0].astype(jnp.bfloat16), tables[1].astype(jnp.bfloat16))
```

```python
import functools

import jax
import jax.numpy as jnp
import numpy as np
from jax import lax
from jax.experimental import pallas as pl
from jax.experimental.pallas import tpu as pltpu
from jax.sharding import PartitionSpec as P

HEAD_SIZE = 128
GROUP = 4
EPS = 1e-06
ROPE_BASE = 1000000.0
LOSS_SCALE = 8192.0
SCALE = HEAD_SIZE ** (-0.5)
BF16 = jnp.bfloat16
F32 = jnp.float32


def dot_nn(a, b):
    return lax.dot_general(a, b, (((1,), (0,)), ((), ())), preferred_element_type=F32)


def dot_nt(a, b):
    return lax.dot_general(a, b, (((1,), (1,)), ((), ())), preferred_element_type=F32)


def dot_tn(a, b):
    return lax.dot_general(a, b, (((0,), (0,)), ((), ())), preferred_element_type=F32)


def z_offsets(nz):
    order = [0]
    for step in range(1, nz // 2 + 1):
        order.append(step)
        if len(order) < nz:
            order.append(-step)
    return order


def main_kernel(
    ny,
    parents,
    visits,
    lengths,
    freq,
    hid,
    upper,
    wq,
    wk,
    wv,
    qgain,
    kgain,
    readout,
    ck,
    cv,
    gh_out,
    got_out,
    par_out,
    w,
    hf,
    cks,
    cvs,
    up,
    urb,
    par,
    par_s,
    kvs,
    kvf,
    acc,
    cosb,
    sinb,
    q,
    own,
    e,
    uv,
    rv,
    lsum,
    asum,
    bsum,
    dv,
    dqt,
    sch,
    scl,
    gs,
    gr,
    g768,
    sib_s,
    sib_r,
    ps,
    rs_s,
    rs_r,
    in_sem,
    par_send,
    par_recv,
    s_sem,
    kv_send,
    kv_recv,
    ag_send,
    ag_recv,
    sch_send,
    sch_recv,
    scl_send,
    scl_recv,
    g_send,
    g_recv,
    sb_send,
    sb_recv,
    rs_send,
    rs_recv,
):
    me_l = lax.axis_index("leaf")
    me_g = lax.axis_index("head")
    nl = lax.axis_size("leaf")
    ng = lax.axis_size("head")
    nz = nl // ny
    nx = ng // 2
    z, y = me_l // ny, me_l % ny
    x, core = me_g // 2, me_g % 2
    nodes, rows, width = ck.shape
    tokens, feats = hid.shape
    half = tokens // 2

    def chip(dx, other=False):
        side = 1 - core if other else core
        return ((x + dx + nx) % nx) * 2 + side

    def leaf_at(dz, dy):
        return ((z + dz + nz) % nz) * ny + (y + dy + ny) % ny

    def remote(src, dst, send, recv, **target):
        return pltpu.make_async_remote_copy(
            src_ref=src,
            dst_ref=dst,
            send_sem=send,
            recv_sem=recv,
            device_id=target,
            device_id_type=pl.DeviceIdType.MESH,
        )

    loads = [
        pltpu.make_async_copy(hid, hf.at[me_g], in_sem.at[0]),
        pltpu.make_async_copy(ck, cks, in_sem.at[1]),
        pltpu.make_async_copy(cv, cvs, in_sem.at[2]),
        pltpu.make_async_copy(wq, w.at[:, pl.ds(0, GROUP * width)], in_sem.at[3]),
        pltpu.make_async_copy(wk, w.at[:, pl.ds(GROUP * width, width)], in_sem.at[4]),
        pltpu.make_async_copy(wv, w.at[:, pl.ds((GROUP + 1) * width, width)], in_sem.at[5]),
        pltpu.make_async_copy(upper, up, in_sem.at[6]),
    ]
    for load in loads:
        load.start()

    barrier = pltpu.get_barrier_semaphore()

    def greet_leaf(o, c):
        pl.semaphore_signal(
            barrier, inc=1, device_id={"leaf": (me_l + o) % nl}, device_id_type=pl.DeviceIdType.MESH
        )
        return c

    def greet_head(o, c):
        pl.semaphore_signal(
            barrier, inc=1, device_id={"head": (me_g + o) % ng}, device_id_type=pl.DeviceIdType.MESH
        )
        return c

    lax.fori_loop(1, nl, greet_leaf, 0)
    lax.fori_loop(1, ng, greet_head, 0)
    lane = lax.broadcasted_iota(jnp.int32, (1, 1, 128), 2)
    par[pl.ds(me_l, 1)] = jnp.where(lane < 64, parents[0], visits[0])
    pl.semaphore_wait(barrier, nl - 1 + ng - 1)

    def par_copy(o):
        return remote(
            par.at[me_l],
            par.at[me_l],
            par_send.at[o],
            par_recv.at[me_l],
            leaf=(me_l + o) % nl,
        )

    def par_start(o, c):
        par_copy(o).start()
        return c

    lax.fori_loop(1, nl, par_start, 0)

    loads[0].wait()

    def ag_copy(sem, block, part, target):
        rows_at = hf.at[block, pl.ds(part * half, half)]
        return remote(rows_at, rows_at, ag_send.at[sem], ag_recv.at[block, part], head=target)

    def ag_wait(block, part):
        rows_at = hf.at[block, pl.ds(part * half, half)]
        remote(rows_at, rows_at, ag_send.at[0], ag_recv.at[block, part], head=me_g).wait_recv()

    right, left, sibling = chip(1), chip(-1), chip(0, True)
    ag = [
        ag_copy(0, me_g, 0, right),
        ag_copy(1, me_g, 1, left),
        ag_copy(2, me_g, 1, right),
        ag_copy(3, me_g, 0, left),
        ag_copy(4, me_g, 0, sibling),
        ag_copy(5, me_g, 1, sibling),
    ]
    for copy in ag:
        copy.start()

    def par_arrive(o, c):
        src = (me_l + o) % nl
        remote(par.at[src], par.at[src], par_send.at[o], par_recv.at[src], leaf=src).wait_recv()
        return c

    lax.fori_loop(1, nl, par_arrive, 0)
    to_smem = pltpu.make_async_copy(par, par_s, s_sem)
    to_smem.start()
    loads[1].wait()
    loads[2].wait()
    to_smem.wait()
    order = z_offsets(nz)
    pairs = [(order[2 * i], order[2 * i + 1]) for i in range(nz // 2)]

    def kv_copy(i, dest):
        return remote(kvs.at[i], kvf.at[me_l], kv_send.at[i], kv_recv.at[me_l], leaf=dest)

    kv_copies = []
    slot = 0
    for dz in order:
        for dy in range(ny):
            dest = leaf_at(-dz, -dy)
            node = par_s[dest, 0, 0]
            if dz == 0 and dy == 0:
                kvf[me_l, 0] = cks[node]
                kvf[me_l, 1] = cvs[node]
            else:
                kvs[slot, 0] = cks[node]
                kvs[slot, 1] = cvs[node]
                copy = kv_copy(slot, dest)
                copy.start()
                kv_copies.append(copy)
                slot += 1

    length = lengths[parents[0]]
    position = (length + lax.broadcasted_iota(jnp.int32, (tokens, width), 0)).astype(F32)
    angle = position * freq[...]
    cosb[...] = jnp.cos(angle)
    low = lax.broadcasted_iota(jnp.int32, (tokens, width), 1) < width // 2
    sine = jnp.sin(angle)
    sinb[...] = jnp.where(low, -sine, sine)

    def rotate(value):
        return value * cosb[...] + pltpu.roll(value, width // 2, 1) * sinb[...]

    def rotate_back(value):
        return value * cosb[...] - pltpu.roll(value, width // 2, 1) * sinb[...]

    loads[6].wait()
    read = readout[...]
    for h in range(GROUP):
        cols = slice(h * width, (h + 1) * width)
        urb[h, :, 0:width] = up[:, cols]
        urb[h, :, width : 2 * width] = jnp.broadcast_to(
            read[:, cols].astype(F32), (tokens, width)
        ).astype(BF16)
    read_rows = jnp.concatenate(
        [read[:, h * width : (h + 1) * width].astype(F32) for h in range(GROUP)]
        + [jnp.zeros((16 - GROUP, width), F32)],
        0,
    ).astype(BF16)

    for i in (3, 4, 5):
        loads[i].wait()

    def project(block, first=False):
        part = dot_nn(hf[block], w[pl.ds(pl.multiple_of(block * feats, feats), feats), :])
        if first:
            acc[...] = part
        else:
            acc[...] += part

    project(me_g, True)
    ag_wait(left, 0)
    more = [ag_copy(6, left, 0, right), ag_copy(7, left, 0, sibling)]
    for copy in more:
        copy.start()
    ag_wait(right, 1)
    more2 = [ag_copy(8, right, 1, left), ag_copy(9, right, 1, sibling)]
    for copy in more2:
        copy.start()
    ag_wait(sibling, 0)
    ag_wait(sibling, 1)
    project(sibling)
    ag_wait(left, 1)
    ag_wait(right, 0)
    more3 = [ag_copy(10, left, 1, sibling), ag_copy(11, right, 0, sibling)]
    for copy in more3:
        copy.start()
    project(left)
    project(right)
    opposite = chip(2)
    ag_wait(opposite, 0)
    more4 = [ag_copy(12, opposite, 0, sibling)]
    more4[0].start()
    ag_wait(opposite, 1)
    more4.append(ag_copy(13, opposite, 1, sibling))
    more4[1].start()
    project(opposite)
    for dx in (-1, 1, 2):
        block = chip(dx, True)
        ag_wait(block, 0)
        ag_wait(block, 1)
        project(block)
    ag += more + more2 + more3 + more4

    def norm_inverse(raw):
        return lax.rsqrt(jnp.mean(raw * raw, axis=-1, keepdims=True) + EPS)

    for h in range(GROUP + 1):
        raw = acc[:, h * width : (h + 1) * width]
        gain = qgain[...] if h < GROUP else kgain[...]
        turned = rotate(raw * norm_inverse(raw) * gain).astype(BF16)
        if h < GROUP:
            q[h] = turned
        else:
            own[0] = turned
    own[1] = acc[:, (GROUP + 1) * width :].astype(BF16)

    def keys_of(i):
        if i == 0:
            return own[0]
        za, zb = [((z + dz + nz) % nz) * ny for dz in pairs[i - 1]]
        return jnp.concatenate(
            [kvf[pl.ds(zz, ny), 0].reshape(ny * rows, width) for zz in (za, zb)], 0
        )

    def values_of(i):
        if i == 0:
            return own[1]
        za, zb = [((z + dz + nz) % nz) * ny for dz in pairs[i - 1]]
        return jnp.concatenate(
            [kvf[pl.ds(zz, ny), 1].reshape(ny * rows, width) for zz in (za, zb)], 0
        )

    chunks = len(pairs) + 1

    def forward(i):
        keys, values = keys_of(i), values_of(i)
        count = keys.shape[0]
        at = lax.broadcasted_iota(jnp.int32, (count, tokens), 0)
        if i == 0:
            mask = at <= lax.broadcasted_iota(jnp.int32, (count, tokens), 1)
        else:
            za, zb = [((z + dz + nz) % nz) * ny * rows for dz in pairs[i - 1]]
            mask = jnp.where(at < ny * rows, at + za, at - ny * rows + zb) < length
        for h in range(GROUP):
            weight = jnp.where(mask, jnp.exp(dot_nt(keys, q[h]) * SCALE), 0.0)
            total = jnp.sum(weight, axis=0, keepdims=True)
            if i == 0:
                lsum[h : h + 1, :] = total
            else:
                lsum[h : h + 1, :] += total
            e[i, h] = weight
            uv[i, h] = dot_nt(values, up[:, h * width : (h + 1) * width])
        rv[i] = dot_nt(values, read_rows)

    forward(0)
    for i in range(1, chunks):
        for dz in pairs[i - 1]:
            for dy in range(ny):
                if dz == 0 and dy == 0:
                    continue
                src = leaf_at(dz, dy)
                remote(
                    kvf.at[src], kvf.at[src], kv_send.at[0], kv_recv.at[src], leaf=src
                ).wait_recv()
        forward(i)

    score = jnp.zeros((1, 1), F32)
    for h in range(GROUP):
        inverse = 1.0 / lsum[h : h + 1, :]
        a = jnp.zeros((1, tokens), F32)
        b = jnp.zeros((1, tokens), F32)
        for i in range(chunks):
            prob = e[i, h] * inverse
            e[i, h] = prob
            a += jnp.sum(prob * rv[i][:, h : h + 1], axis=0, keepdims=True)
            b += jnp.sum(prob * uv[i, h], axis=0, keepdims=True)
        asum[h : h + 1, :] = a
        bsum[h : h + 1, :] = b
        score += jnp.sum(a, axis=1, keepdims=True)
    sch[pl.ds(me_g, 1)] = jnp.broadcast_to((score / tokens)[None], (1, 1, 128))

    def sch_copy(o):
        return remote(
            sch.at[me_g], sch.at[me_g], sch_send.at[o], sch_recv.at[me_g], head=(me_g + o) % ng
        )

    def scl_copy(o):
        return remote(
            scl.at[me_l], scl.at[me_l], scl_send.at[o], scl_recv.at[me_l], leaf=(me_l + o) % nl
        )

    for o in range(1, ng):
        sch_copy(o).start()

    def value_grads(i):
        total = None
        for h in range(GROUP):
            term = dot_nn(e[i, h].astype(BF16), urb[h])
            total = term if total is None else total + term
        dv[i] = total

    for i in range(chunks // 2):
        value_grads(i)
    for o in range(1, ng):
        src = (me_g + o) % ng
        remote(sch.at[src], sch.at[src], sch_send.at[o], sch_recv.at[src], head=src).wait_recv()
    scl[pl.ds(me_l, 1)] = jnp.sum(sch[...], axis=0, keepdims=True)

    def scl_start(o, c):
        scl_copy(o).start()
        return c

    lax.fori_loop(1, nl, scl_start, 0)
    for i in range(chunks // 2, chunks):
        value_grads(i)

    def scl_arrive(o, c):
        src = (me_l + o) % nl
        remote(scl.at[src], scl.at[src], scl_send.at[o], scl_recv.at[src], leaf=src).wait_recv()
        return c

    lax.fori_loop(1, nl, scl_arrive, 0)

    node_at = lax.broadcasted_iota(jnp.int32, (nl, 1, 128), 2)
    table = par[...]
    hot = jnp.where(table == node_at, 1.0, 0.0) * jnp.where(node_at < nodes, 1.0, 0.0)
    seen = pltpu.roll(table.reshape(nl, 128), 64, 1).reshape(nl, 1, 128).astype(F32)
    seen = jnp.sum(jnp.where(node_at == 0, seen, 0.0), axis=2, keepdims=True)
    grown = jnp.exp(scl[...])
    node_total = jnp.sum(hot * grown, axis=0, keepdims=True)
    node_seen = jnp.sum(hot * seen, axis=0, keepdims=True)
    mine = (lax.broadcasted_iota(jnp.int32, (nl, 1, 128), 0) == me_l).astype(F32)
    own_hot = jnp.sum(hot * mine, axis=0)
    own_total = jnp.sum(own_hot * node_total[0], axis=1, keepdims=True)
    own_seen = jnp.sum(own_hot * node_seen[0], axis=1, keepdims=True)
    own_grown = jnp.sum(jnp.where(lane[0] == 0, jnp.sum(grown * mine, axis=0), 0.0), axis=1, keepdims=True)
    own_visits = jnp.sum(jnp.where(lane[0] == 0, jnp.sum(seen * mine, axis=0), 0.0), axis=1, keepdims=True)
    c = (LOSS_SCALE / tokens) * (own_grown / own_total - own_visits / own_seen)

    g_copies = []
    for i in list(range(1, chunks)) + [0]:
        keys = keys_of(i)
        grad_keys = None
        for h in range(GROUP):
            shift = bsum[h : h + 1, :] + c * asum[h : h + 1, :]
            grad = uv[i, h] + c * rv[i][:, h : h + 1] - shift
            grad = (e[i, h] * grad * SCALE).astype(BF16)
            term = dot_nn(grad, q[h])
            grad_keys = term if grad_keys is None else grad_keys + term
            back = dot_tn(keys, grad)
            if i == 1:
                dqt[h] = back
            else:
                dqt[h] += back
        grad_values = dv[i][:, :width] + c * dv[i][:, width:]
        if i == 0:
            step_grad_keys, step_grad_values = grad_keys, grad_values
            continue
        for j, dz in enumerate(pairs[i - 1]):
            zz = ((z + dz + nz) % nz) * ny
            part = slice(j * ny * rows, (j + 1) * ny * rows)
            gs[pl.ds(zz, ny), 0] = grad_keys[part].astype(BF16).reshape(ny, rows, width)
            gs[pl.ds(zz, ny), 1] = grad_values[part].astype(BF16).reshape(ny, rows, width)
            for dy in range(ny):
                dest = leaf_at(dz, dy)
                if dz == 0 and dy == 0:
                    gr[me_l] = gs[me_l]
                else:
                    copy = remote(
                        gs.at[dest], gr.at[me_l], g_send.at[len(g_copies)], g_recv.at[me_l], leaf=dest
                    )
                    copy.start()
                    g_copies.append(copy)

    def norm_back(raw, gain, grad):
        inverse = norm_inverse(raw)
        scaled = grad * gain
        mean = jnp.mean(raw * scaled, axis=-1, keepdims=True)
        return (inverse * scaled - raw * (inverse * inverse * inverse) * mean).astype(BF16)

    for h in range(GROUP):
        cols = slice(h * width, (h + 1) * width)
        g768[:, cols] = norm_back(acc[:, cols], qgain[...], rotate_back(dqt[h].T))
    cols = slice(GROUP * width, (GROUP + 1) * width)
    g768[:, cols] = norm_back(acc[:, cols], kgain[...], rotate_back(step_grad_keys))
    g768[:, (GROUP + 1) * width :] = step_grad_values.astype(BF16)

    def term(block):
        return dot_nt(g768[...], w[pl.ds(pl.multiple_of(block * feats, feats), feats), :])

    sb_copies = []
    hops = (2, 1, -1, 0)
    for j, dx in enumerate(hops):
        sib_s[j] = term(chip(dx, True)).astype(BF16)
        copy = remote(sib_s.at[j], sib_r.at[j], sb_send.at[j], sb_recv.at[j], head=sibling)
        copy.start()
        sb_copies.append(copy)
        ps[j] = term(chip(dx)).astype(BF16).astype(F32)

    def join(j):
        remote(sib_s.at[j], sib_r.at[j], sb_send.at[j], sb_recv.at[j], head=sibling).wait_recv()
        ps[j] += sib_r[j].astype(F32)

    def rs_copy(slot, target):
        return remote(rs_s.at[slot], rs_r.at[slot], rs_send.at[slot], rs_recv.at[slot], head=target)

    first, second = slice(0, half), slice(half, tokens)
    join(0)
    rs_s[0] = ps[0, first].astype(BF16)
    rs_s[1] = ps[0, second].astype(BF16)
    rs_copies = [rs_copy(0, right), rs_copy(1, left)]
    rs_copies[0].start()
    rs_copies[1].start()
    join(1)
    rs_s[2] = ps[1, second].astype(BF16)
    rs_copies.append(rs_copy(2, right))
    rs_copies[2].start()
    join(2)
    rs_s[3] = ps[2, first].astype(BF16)
    rs_copies.append(rs_copy(3, left))
    rs_copies[3].start()
    rs_copies[0].wait_recv()
    rs_s[4] = (ps[1, first] + rs_r[0].astype(F32)).astype(BF16)
    rs_copies.append(rs_copy(4, right))
    rs_copies[4].start()
    rs_copies[1].wait_recv()
    rs_s[5] = (ps[2, second] + rs_r[1].astype(F32)).astype(BF16)
    rs_copies.append(rs_copy(5, left))
    rs_copies[5].start()
    join(3)
    for slot in range(2, 6):
        rs_copies[slot].wait_recv()
    gh_out[first, :] = (ps[3, first] + rs_r[4].astype(F32) + rs_r[3].astype(F32)).astype(BF16)
    gh_out[second, :] = (ps[3, second] + rs_r[2].astype(F32) + rs_r[5].astype(F32)).astype(BF16)

    for dz in order:
        for dy in range(ny):
            if dz == 0 and dy == 0:
                continue
            src = leaf_at(-dz, -dy)
            remote(gr.at[src], gr.at[src], g_send.at[0], g_recv.at[src], leaf=src).wait_recv()
    got_out[...] = gr[...]
    par_out[...] = par[...]

    for copy in ag + kv_copies + sb_copies + rs_copies + g_copies:
        copy.wait_send()
    for o in range(1, ng):
        sch_copy(o).wait_send()

    def small_sent(o, c):
        par_copy(o).wait_send()
        scl_copy(o).wait_send()
        return c

    lax.fori_loop(1, nl, small_sent, 0)


def collect_kernel(par, got, gh_in, gh, gk, gv, total):
    total[...] = jnp.zeros_like(total)

    def add(s, c):
        node = par[s, 0, 0]
        total[node] += got[s].astype(F32)
        return c

    lax.fori_loop(0, got.shape[0], add, 0)
    gk[...] = total[:, 0].astype(BF16)
    gv[...] = total[:, 1].astype(BF16)
    gh[...] = gh_in[...]


def per_device(
    ny,
    hidden_states,
    upper_gradient,
    w_query,
    key_projection,
    value_projection,
    query_gain,
    key_norm_gain,
    readout,
    cached_prefix_keys,
    cached_prefix_values,
    prefix_lengths,
    parents,
    visits,
):
    nl, ng = lax.axis_size("leaf"), lax.axis_size("head")
    nodes, rows, width = cached_prefix_keys.shape
    tokens, feats = hidden_states.shape
    model = w_query.shape[0]
    nz = nl // ny
    chunks = nz // 2 + 1
    span = max(2 * ny * rows, tokens)
    half = tokens // 2
    cols = (GROUP + 2) * width
    inverse = np.asarray(
        ROPE_BASE ** (-2.0 * (np.arange(width) % (width // 2)) / width), np.float32
    ).reshape(1, width)
    smem = pl.BlockSpec(memory_space=pltpu.SMEM)
    vmem = pl.BlockSpec(memory_space=pltpu.VMEM)
    anywhere = pl.BlockSpec(memory_space=pl.ANY)
    dma = pltpu.SemaphoreType.DMA
    scratch = [
        pltpu.VMEM((model, cols), BF16),
        pltpu.VMEM((ng, tokens, feats), BF16),
        pltpu.VMEM((nodes, rows, width), BF16),
        pltpu.VMEM((nodes, rows, width), BF16),
        pltpu.VMEM((tokens, GROUP * width), BF16),
        pltpu.VMEM((GROUP, tokens, 2 * width), BF16),
        pltpu.VMEM((nl, 1, 128), jnp.int32),
        pltpu.SMEM((nl, 1, 128), jnp.int32),
        pltpu.VMEM((nl, 2, rows, width), BF16),
        pltpu.VMEM((nl, 2, rows, width), BF16),
        pltpu.VMEM((tokens, cols), F32),
        pltpu.VMEM((tokens, width), F32),
        pltpu.VMEM((tokens, width), F32),
        pltpu.VMEM((GROUP, tokens, width), BF16),
        pltpu.VMEM((2, tokens, width), BF16),
        pltpu.VMEM((chunks, GROUP, span, tokens), F32),
        pltpu.VMEM((chunks, GROUP, span, tokens), F32),
        pltpu.VMEM((chunks, span, 16), F32),
        pltpu.VMEM((GROUP, tokens), F32),
        pltpu.VMEM((GROUP, tokens), F32),
        pltpu.VMEM((GROUP, tokens), F32),
        pltpu.VMEM((chunks, span, 2 * width), F32),
        pltpu.VMEM((GROUP, width, tokens), F32),
        pltpu.VMEM((ng, 1, 128), F32),
        pltpu.VMEM((nl, 1, 128), F32),
        pltpu.VMEM((nl, 2, rows, width), BF16),
        pltpu.VMEM((nl, 2, rows, width), BF16),
        pltpu.VMEM((tokens, cols), BF16),
        pltpu.VMEM((4, tokens, feats), BF16),
        pltpu.VMEM((4, tokens, feats), BF16),
        pltpu.VMEM((4, tokens, feats), F32),
        pltpu.VMEM((6, half, feats), BF16),
        pltpu.VMEM((6, half, feats), BF16),
        dma((7,)),
        dma((nl,)),
        dma((nl,)),
        dma,
        dma((nl,)),
        dma((nl,)),
        dma((14,)),
        dma((ng, 2)),
        dma((ng,)),
        dma((ng,)),
        dma((nl,)),
        dma((nl,)),
        dma((nl,)),
        dma((nl,)),
        dma((4,)),
        dma((4,)),
        dma((6,)),
        dma((6,)),
    ]
    gh, got, par = pl.pallas_call(
        functools.partial(main_kernel, ny),
        out_shape=(
            jax.ShapeDtypeStruct((tokens, feats), BF16),
            jax.ShapeDtypeStruct((nl, 2, rows, width), BF16),
            jax.ShapeDtypeStruct((nl, 1, 128), jnp.int32),
        ),
        in_specs=[smem, smem, smem, vmem]
        + [anywhere] * 5
        + [vmem] * 3
        + [anywhere] * 2,
        out_specs=(vmem, vmem, vmem),
        scratch_shapes=scratch,
        compiler_params=pltpu.CompilerParams(
            collective_id=0, has_side_effects=True, vmem_limit_bytes=58 * 1024 * 1024
        ),
    )(
        parents,
        visits,
        prefix_lengths,
        jnp.asarray(inverse),
        hidden_states,
        upper_gradient,
        w_query,
        key_projection,
        value_projection,
        query_gain.reshape(1, width),
        key_norm_gain.reshape(1, width),
        readout.reshape(1, GROUP * width),
        cached_prefix_keys,
        cached_prefix_values,
    )
    table = jax.ShapeDtypeStruct((nodes, rows, width), BF16)
    return pl.pallas_call(
        collect_kernel,
        out_shape=(jax.ShapeDtypeStruct((tokens, feats), BF16), table, table),
        in_specs=[smem, vmem, vmem],
        out_specs=(vmem, vmem, vmem),
        scratch_shapes=[pltpu.VMEM((nodes, 2, rows, width), F32)],
    )(par, got, gh)


def solution(mesh):
    in_specs = (
        P("leaf", "head"),
        P("leaf", "head"),
        P(None, "head"),
        P(None, "head"),
        P(None, "head"),
        P(),
        P(),
        P("head"),
        P(None, "leaf", "head"),
        P(None, "leaf", "head"),
        P(),
        P("leaf"),
        P("leaf"),
    )
    out_specs = (P("leaf", "head"), P(None, "leaf", "head"), P(None, "leaf", "head"))
    ny = 4 if mesh.shape["leaf"] == 32 else 1
    return jax.shard_map(
        functools.partial(per_device, ny),
        mesh=mesh,
        in_specs=in_specs,
        out_specs=out_specs,
        check_vma=False,
    )
```

```python
import functools

import jax
import jax.numpy as jnp
import numpy as np
from jax import lax
from jax.experimental import pallas as pl
from jax.experimental.pallas import tpu as pltpu
from jax.sharding import PartitionSpec as P

HEAD_SIZE = 128
GROUP = 4
EPS = 1e-06
ROPE_BASE = 1000000.0
LOSS_SCALE = 8192.0
SCALE = HEAD_SIZE ** (-0.5)
BF16 = jnp.bfloat16
F32 = jnp.float32


def dot_nn(a, b):
    return lax.dot_general(a, b, (((1,), (0,)), ((), ())), preferred_element_type=F32)


def dot_nt(a, b):
    return lax.dot_general(a, b, (((1,), (1,)), ((), ())), preferred_element_type=F32)


def dot_tn(a, b):
    return lax.dot_general(a, b, (((0,), (0,)), ((), ())), preferred_element_type=F32)


def slot_offsets(nz, ny):
    order = [0]
    for step in range(1, nz // 2 + 1):
        order.append(step)
        if len(order) < nz:
            order.append(-step)
    return [(dz, dy) for dz in order for dy in range(ny)]


def main_kernel(
    ny,
    parents,
    visits,
    lengths,
    freq,
    hid,
    upper,
    wq,
    wk,
    wv,
    qgain,
    kgain,
    readout,
    ck,
    cv,
    gh_out,
    dk_out,
    dv_out,
    cw_out,
    par_out,
    w,
    wsib,
    hf,
    cks,
    cvs,
    up,
    ue,
    par,
    par_s,
    hot,
    seen,
    kvs,
    kvf,
    acc,
    cosb,
    sinb,
    q,
    own,
    e,
    uv,
    rv,
    lsum,
    asum,
    bsum,
    tops,
    dv,
    gl,
    sch,
    sls,
    scl,
    dvs,
    dvr,
    dks,
    dkr,
    gx,
    gxr,
    gg,
    ps,
    rs_s,
    rs_r,
    in_sem,
    par_send,
    par_recv,
    s_sem,
    kv_send,
    kv_recv,
    ag_send,
    ag_recv,
    ws_send,
    ws_recv,
    sch_send,
    sch_recv,
    scl_send,
    scl_recv,
    dv_send,
    dv_recv,
    dk_send,
    dk_recv,
    gx_send,
    gx_recv,
    rs_send,
    rs_recv,
):
    me_l = lax.axis_index("leaf")
    me_g = lax.axis_index("head")
    nl = lax.axis_size("leaf")
    ng = lax.axis_size("head")
    nz = nl // ny
    nx = ng // 2
    z, y = me_l // ny, me_l % ny
    x, core = me_g // 2, me_g % 2
    nodes, rows, width = ck.shape
    tokens, feats = hid.shape
    half = tokens // 2
    offsets = slot_offsets(nz, ny)
    place = {(dz % nz, dy): slot for slot, (dz, dy) in enumerate(offsets)}
    mirror = [place[(-dz % nz, -dy % ny)] for dz, dy in offsets]
    per = 2 * ny
    chunks = nl // per

    def chip(dx, other=False):
        side = 1 - core if other else core
        return ((x + dx + nx) % nx) * 2 + side

    def leaf_of(slot):
        dz, dy = offsets[slot]
        return ((z + dz + nz) % nz) * ny + (y + dy) % ny

    def remote(src, dst, send, recv, **target):
        return pltpu.make_async_remote_copy(
            src_ref=src,
            dst_ref=dst,
            send_sem=send,
            recv_sem=recv,
            device_id=target,
            device_id_type=pl.DeviceIdType.MESH,
        )

    loads = [
        pltpu.make_async_copy(hid, hf.at[me_g], in_sem.at[0]),
        pltpu.make_async_copy(ck, cks, in_sem.at[1]),
        pltpu.make_async_copy(cv, cvs, in_sem.at[2]),
        pltpu.make_async_copy(wq, w.at[:, pl.ds(0, GROUP * width)], in_sem.at[3]),
        pltpu.make_async_copy(wk, w.at[:, pl.ds(GROUP * width, width)], in_sem.at[4]),
        pltpu.make_async_copy(wv, w.at[:, pl.ds((GROUP + 1) * width, width)], in_sem.at[5]),
        pltpu.make_async_copy(upper, up, in_sem.at[6]),
    ]
    for load in loads:
        load.start()

    barrier = pltpu.get_barrier_semaphore()
    for o in range(1, nl):
        pl.semaphore_signal(
            barrier, inc=1, device_id={"leaf": (me_l + o) % nl}, device_id_type=pl.DeviceIdType.MESH
        )
    for o in range(1, ng):
        pl.semaphore_signal(
            barrier, inc=1, device_id={"head": (me_g + o) % ng}, device_id_type=pl.DeviceIdType.MESH
        )
    lane = lax.broadcasted_iota(jnp.int32, (1, 128), 1)
    par[pl.ds(me_l, 1)] = jnp.where(lane == 0, parents[0], visits[0]).reshape(1, 1, 128)
    pl.semaphore_wait(barrier, nl - 1 + ng - 1)

    for o in range(1, nl):
        remote(
            par.at[me_l], par.at[me_l], par_send, par_recv, leaf=(me_l + o) % nl
        ).start()

    loads[0].wait()

    def ag_copy(sem, block, part, target):
        rows_at = hf.at[block, pl.ds(part * half, half)]
        return remote(rows_at, rows_at, ag_send.at[sem], ag_recv.at[block, part], head=target)

    def ag_wait(block, part):
        rows_at = hf.at[block, pl.ds(part * half, half)]
        remote(rows_at, rows_at, ag_send.at[0], ag_recv.at[block, part], head=me_g).wait_recv()

    right, left, sibling = chip(1), chip(-1), chip(0, True)
    ag = [
        ag_copy(0, me_g, 0, right),
        ag_copy(1, me_g, 1, left),
        ag_copy(2, me_g, 1, right),
        ag_copy(3, me_g, 0, left),
        ag_copy(4, me_g, 0, sibling),
        ag_copy(5, me_g, 1, sibling),
    ]
    for copy in ag:
        copy.start()

    loads[1].wait()
    loads[2].wait()
    some = par.at[pl.ds(0, nl - 1)]
    remote(some, some, par_send, par_recv, leaf=me_l).wait_recv()
    to_smem = pltpu.make_async_copy(par, par_s, s_sem)
    to_smem.start()
    to_smem.wait()
    for slot in range(nl):
        there = mirror[slot]
        dest = leaf_of(there)
        node = par_s[dest, 0, 0]
        if slot == 0:
            kvf[0, 0] = cks[node]
            kvf[0, 1] = cvs[node]
        else:
            kvs[slot, 0] = cks[node]
            kvs[slot, 1] = cvs[node]
            remote(
                kvs.at[slot], kvf.at[slot], kv_send, kv_recv.at[slot // per], leaf=dest
            ).start()

    for slot in range(nl):
        src = leaf_of(slot)
        par_out[slot] = jnp.full((1, 128), par_s[src, 0, 0], jnp.int32)
        hot[slot] = jnp.where((lane == par_s[src, 0, 0]) & (lane < nodes), 1.0, 0.0)
        seen[slot] = jnp.full((1, 128), par_s[src, 0, 1], jnp.int32).astype(F32)

    length = lengths[parents[0]]
    position = (length + lax.broadcasted_iota(jnp.int32, (tokens, width), 0)).astype(F32)
    angle = position * freq[...]
    cosb[...] = jnp.cos(angle)
    low = lax.broadcasted_iota(jnp.int32, (tokens, width), 1) < width // 2
    sine = jnp.sin(angle)
    sinb[...] = jnp.where(low, -sine, sine)

    def rotate(value):
        return value * cosb[...] + pltpu.roll(value, width // 2, 1) * sinb[...]

    def rotate_back(value):
        return value * cosb[...] - pltpu.roll(value, width // 2, 1) * sinb[...]

    loads[6].wait()
    at_lane = lax.broadcasted_iota(jnp.int32, (tokens, width), 1)
    for h in range(GROUP):
        ue[h, :, 0:width] = up[:, h * width : (h + 1) * width]
        ue[h, :, width : 2 * width] = jnp.where(at_lane == h, 1.0, 0.0).astype(BF16)
    read = [readout[h * width : (h + 1) * width].astype(F32).reshape(1, width) for h in range(GROUP)]
    read_rows = jnp.concatenate(read + [jnp.zeros((16 - GROUP, width), F32)], 0).astype(BF16)

    for i in (3, 4, 5):
        loads[i].wait()

    def block_rows(block):
        return pl.ds(pl.multiple_of(block * feats, feats), feats)

    def project(block, first=False):
        part = dot_nn(hf[block], w[block_rows(block), :])
        if first:
            acc[...] = part
        else:
            acc[...] += part

    def keys_of(i, which=0):
        if i == chunks:
            return own[which]
        return kvf[pl.ds(i * per, per), which].reshape(per * rows, width)

    def wait_rows(i):
        skip = 1 if i == 0 else 0
        some = kvf.at[pl.ds(i * per + skip, per - skip)]
        remote(some, some, kv_send, kv_recv.at[i], leaf=me_l).wait_recv()

    def values_product(i):
        values = keys_of(i, 1)
        for h in range(GROUP):
            uv[i, h] = dot_nt(values, up[:, h * width : (h + 1) * width])
        rv[i] = dot_nt(values, read_rows)

    project(me_g, True)

    def pass_on(*copies):
        for copy in copies:
            copy.start()
            ag.append(copy)

    ag_wait(left, 0)
    pass_on(ag_copy(6, left, 0, right), ag_copy(7, left, 0, sibling))
    ag_wait(right, 1)
    pass_on(ag_copy(8, right, 1, left), ag_copy(9, right, 1, sibling))
    ag_wait(sibling, 0)
    ag_wait(sibling, 1)
    project(sibling)
    ag_wait(left, 1)
    ag_wait(right, 0)
    pass_on(ag_copy(10, left, 1, sibling), ag_copy(11, right, 0, sibling))
    project(left)
    project(right)

    def project_other(dx):
        block = chip(dx, True)
        ag_wait(block, 0)
        ag_wait(block, 1)
        project(block)

    project_other(-1)
    project_other(1)
    wait_rows(0)
    values_product(0)
    opposite = chip(2)
    ag_wait(opposite, 0)
    pass_on(ag_copy(12, opposite, 0, sibling))
    ag_wait(opposite, 1)
    pass_on(ag_copy(13, opposite, 1, sibling))
    project(opposite)
    project_other(2)

    hops = (2, 1, -1, 0)
    ws_copies = []
    for j, dx in enumerate(hops):
        copy = remote(
            w.at[block_rows(chip(dx, True))], wsib.at[j], ws_send.at[j], ws_recv.at[j], head=sibling
        )
        copy.start()
        ws_copies.append(copy)

    def norm_inverse(raw):
        return lax.rsqrt(jnp.mean(raw * raw, axis=-1, keepdims=True) + EPS)

    for h in range(GROUP + 1):
        raw = acc[:, h * width : (h + 1) * width]
        gain = qgain[...] if h < GROUP else kgain[...]
        turned = rotate(raw * norm_inverse(raw) * gain).astype(BF16)
        if h < GROUP:
            q[h] = turned
        else:
            own[0] = turned
    own[1] = acc[:, (GROUP + 1) * width :].astype(BF16)

    def forward(i, first):
        keys = keys_of(i)
        if i == chunks:
            shape = (tokens, tokens)
            mask = lax.broadcasted_iota(jnp.int32, shape, 0) <= lax.broadcasted_iota(
                jnp.int32, shape, 1
            )
        else:
            at = lax.broadcasted_iota(jnp.int32, (rows, tokens), 0)
            mask = (
                jnp.concatenate([at + leaf_of(i * per + b) * rows for b in range(per)], 0) < length
            )
        for h in range(GROUP):
            logits = jnp.where(mask, dot_nt(keys, q[h]) * SCALE, -1e30)
            top = jnp.max(logits, axis=0, keepdims=True)
            if not first:
                before = tops[i_last[0], h : h + 1, :]
                top = jnp.maximum(top, before)
            weight = jnp.exp(logits - top)
            total = jnp.sum(weight, axis=0, keepdims=True)
            a = jnp.sum(weight * rv[i][:, h : h + 1], axis=0, keepdims=True)
            if not first:
                fade = jnp.exp(before - top)
                total += lsum[h : h + 1, :] * fade
                a += asum[h : h + 1, :] * fade
            lsum[h : h + 1, :] = total
            asum[h : h + 1, :] = a
            tops[i, h : h + 1, :] = top
            e[i, h] = weight
        i_last[0] = i

    i_last = [None]
    values_product(chunks)
    forward(chunks, True)
    forward(0, False)
    for i in range(1, chunks):
        wait_rows(i)
        values_product(i)
        forward(i, False)

    score = jnp.zeros((1, 1), F32)
    for h in range(GROUP):
        inverse = 1.0 / lsum[h : h + 1, :]
        lsum[h : h + 1, :] = inverse
        a = asum[h : h + 1, :] * inverse
        asum[h : h + 1, :] = a
        score += jnp.sum(a, axis=1, keepdims=True)
    sch[0] = jnp.broadcast_to(score / tokens, (1, 128))
    for o in range(1, ng):
        remote(sch.at[0], sch.at[o], sch_send, sch_recv, head=(me_g + o) % ng).start()

    for h in range(GROUP):
        b = jnp.zeros((1, tokens), F32)
        for i in range(chunks + 1):
            factor = lsum[h : h + 1, :]
            if i != chunks - 1:
                factor *= jnp.exp(tops[i, h : h + 1, :] - tops[chunks - 1, h : h + 1, :])
            prob = e[i, h] * factor
            e[i, h] = prob
            b += jnp.sum(prob * uv[i, h], axis=0, keepdims=True)
            term = dot_nn(prob.astype(BF16), ue[h])
            if h == 0:
                dv[i] = term
            else:
                dv[i] += term
        bsum[h : h + 1, :] = b

    def send_rows(buffer, target, send, recv, slot):
        remote(buffer.at[slot], target.at[mirror[slot]], send, recv, leaf=leaf_of(slot)).start()

    def send_values(i):
        dvs[pl.ds(i * per, per)] = dv[i][:, :width].astype(BF16).reshape(per, rows, width)
        for slot in range(i * per, (i + 1) * per):
            if slot == 0:
                dvr[0] = dvs[0]
            else:
                send_rows(dvs, dvr, dv_send, dv_recv, slot)

    for i in range(chunks // 2):
        send_values(i)

    parts = 128 // rows
    group = lane // rows
    diagonal = lax.broadcasted_iota(jnp.int32, (8, 128), 0) == lax.broadcasted_iota(
        jnp.int32, (8, 128), 1
    ) // rows
    for i in range(chunks):
        sums = dv[i][:, width:].T[0:8]
        for j in range(per // parts):
            tile = sums[:, j * 128 : (j + 1) * 128]
            turns = []
            for k in range(parts):
                moved = tile if k == 0 else pltpu.roll(tile, rows * k, 1)
                turns.append(jnp.sum(jnp.where(diagonal, moved, 0.0), axis=0, keepdims=True))
            for b in range(parts):
                line = turns[(0 - b) % parts]
                for h in range(1, parts):
                    line = jnp.where(group == h, turns[(h - b) % parts], line)
                sls[i * per + j * parts + b, 1:2] = line

    def norm_back(raw, gain, grad):
        inverse = norm_inverse(raw)
        scaled = grad * gain
        mean = jnp.mean(raw * scaled, axis=-1, keepdims=True)
        return (inverse * scaled - raw * (inverse * inverse * inverse) * mean).astype(BF16)

    gx_copies = [
        remote(gx.at[j], gxr.at[j], gx_send.at[j], gx_recv.at[j], head=sibling)
        for j in range(GROUP + 2)
    ]

    def query_grads(h):
        for part in range(2):
            back = None
            for i in range(chunks + 1):
                prob = e[i, h] * SCALE
                if part == 0:
                    grad = uv[i, h] - bsum[h : h + 1, :]
                else:
                    grad = rv[i][:, h : h + 1] - asum[h : h + 1, :]
                grad = (prob * grad).astype(BF16)
                gl[part, i, h] = grad
                term = dot_tn(keys_of(i), grad)
                back = term if back is None else back + term
            gx[h, part] = norm_back(
                acc[:, h * width : (h + 1) * width], qgain[...], rotate_back(back.T)
            )
        gx_copies[h].start()

    query_grads(0)

    some = sch.at[pl.ds(1, ng - 1)]
    remote(some, some, sch_send, sch_recv, head=me_g).wait_recv()
    step_score = jnp.sum(sch[...], axis=0)
    for slot in range(nl):
        sls[slot, 0:1] = step_score
    scl[0] = sls[0]
    for slot in range(1, nl):
        send_rows(sls, scl, scl_send, scl_recv, slot)
    for i in range(chunks // 2, chunks):
        send_values(i)
    for h in range(1, GROUP):
        query_grads(h)

    read_value = None
    for h in range(GROUP):
        term = dv[chunks][:, width + h : width + h + 1] * read[h]
        read_value = term if read_value is None else read_value + term
    gx[GROUP + 1, 0] = dv[chunks][:, :width].astype(BF16)
    gx[GROUP + 1, 1] = read_value.astype(BF16)
    gx_copies[GROUP + 1].start()
    for part in range(2):
        back = None
        for h in range(GROUP):
            term = dot_nn(gl[part, chunks, h], q[h])
            back = term if back is None else back + term
        cols = slice(GROUP * width, (GROUP + 1) * width)
        gx[GROUP, part] = norm_back(acc[:, cols], kgain[...], rotate_back(back))
    gx_copies[GROUP].start()

    some = scl.at[pl.ds(1, nl - 1)]
    remote(some, some, scl_send, scl_recv, leaf=me_l).wait_recv()
    match = hot[...]
    grown = jnp.exp(scl[:, 0:1, :])
    count = seen[...]
    node_total = jnp.sum(match * grown, axis=0, keepdims=True)
    node_seen = jnp.sum(match * count, axis=0, keepdims=True)
    total = jnp.sum(match * node_total, axis=2, keepdims=True)
    total_seen = jnp.sum(match * node_seen, axis=2, keepdims=True)
    scales = (LOSS_SCALE / tokens) * (grown / total - count / total_seen)
    cw_out[...] = scales * scl[:, 1:2, :]
    scale = scales[0, :, 0:1]

    for j in range(GROUP + 2):
        cols = slice(j * width, (j + 1) * width)
        gg[0, :, cols] = (gx[j, 0].astype(F32) + scale * gx[j, 1].astype(F32)).astype(BF16)
    for j in range(GROUP + 2):
        cols = slice(j * width, (j + 1) * width)
        gx_copies[j].wait_recv()
        gg[1, :, cols] = (gxr[j, 0].astype(F32) + scale * gxr[j, 1].astype(F32)).astype(BF16)

    def term(j):
        ws_copies[j].wait_recv()
        ps[j] = dot_nt(gg[0], w[block_rows(chip(hops[j])), :]) + dot_nt(gg[1], wsib[j])

    rs_copies = []

    def rs_send_rows(value, target):
        slot = len(rs_copies)
        rs_s[slot] = value.astype(BF16)
        copy = remote(
            rs_s.at[slot], rs_r.at[slot], rs_send.at[slot], rs_recv.at[slot], head=target
        )
        copy.start()
        rs_copies.append(copy)

    first, second = slice(0, half), slice(half, tokens)
    term(0)
    rs_send_rows(ps[0, first], right)
    rs_send_rows(ps[0, second], left)

    def send_keys(i):
        total = None
        for h in range(GROUP):
            grad = gl[0, i, h].astype(F32) + scale * gl[1, i, h].astype(F32)
            part = dot_nn(grad.astype(BF16), q[h])
            total = part if total is None else total + part
        dks[pl.ds(i * per, per)] = total.astype(BF16).reshape(per, rows, width)
        for slot in range(i * per, (i + 1) * per):
            if slot == 0:
                dkr[0] = dks[0]
            else:
                send_rows(dks, dkr, dk_send, dk_recv, slot)

    for i in range(chunks // 2):
        send_keys(i)
    term(1)
    rs_send_rows(ps[1, second], right)
    term(2)
    rs_send_rows(ps[2, first], left)
    for i in range(chunks // 2, chunks):
        send_keys(i)
    rs_copies[0].wait_recv()
    rs_send_rows(ps[1, first] + rs_r[0].astype(F32), right)
    rs_copies[1].wait_recv()
    rs_send_rows(ps[2, second] + rs_r[1].astype(F32), left)
    term(3)

    some = dvr.at[pl.ds(1, nl - 1)]
    remote(some, some, dv_send, dv_recv, leaf=me_l).wait_recv()
    dv_out[...] = dvr[...]
    remote(some, some, dk_send, dk_recv, leaf=me_l).wait_recv()
    dk_out[...] = dkr[...]

    for slot in range(2, 6):
        rs_copies[slot].wait_recv()
    gh_out[first, :] = (ps[3, first] + rs_r[4].astype(F32) + rs_r[3].astype(F32)).astype(BF16)
    gh_out[second, :] = (ps[3, second] + rs_r[2].astype(F32) + rs_r[5].astype(F32)).astype(BF16)

    for copy in ag + ws_copies + gx_copies + rs_copies:
        copy.wait_send()
    for buffer, send, recv in (
        (par, par_send, par_recv),
        (kvs, kv_send, kv_recv.at[0]),
        (dvs, dv_send, dv_recv),
        (dks, dk_send, dk_recv),
        (sls, scl_send, scl_recv),
    ):
        some = buffer.at[pl.ds(0, nl - 1)]
        remote(some, some, send, recv, leaf=me_l).wait_send()
    some = sch.at[pl.ds(1, ng - 1)]
    remote(some, some, sch_send, sch_recv, head=me_g).wait_send()


def collect_kernel(par, readout, dk_in, dv_in, cw, gh_in, gh, gk, gv, key_total, value_total, sums):
    nodes, rows, width = gk.shape
    key_total[...] = jnp.zeros_like(key_total)
    value_total[...] = jnp.zeros_like(value_total)
    sums[...] = jnp.zeros_like(sums)

    def add(s, c):
        node = par[s, 0, 0]
        key_total[node] += dk_in[s].astype(F32)
        value_total[node] += dv_in[s].astype(F32)
        sums[node] += cw[s]
        return c

    lax.fori_loop(0, dk_in.shape[0], add, 0)
    gk[...] = key_total[...].astype(BF16)
    shape = (1, rows, 128)
    keep = lax.broadcasted_iota(jnp.int32, shape, 2) % rows == lax.broadcasted_iota(
        jnp.int32, shape, 1
    )
    left = jnp.where(keep, sums[...], 0.0).reshape(nodes * rows, 128)
    high = left.astype(BF16)
    rest = (left - high.astype(F32)).astype(BF16)
    right = jnp.concatenate(
        [
            jnp.broadcast_to(
                readout[h * width : (h + 1) * width].astype(F32).reshape(1, width), (rows, width)
            )
            for h in range(128 // rows)
        ],
        0,
    ).astype(BF16)
    extra = dot_nn(high, right) + dot_nn(rest, right)
    gv[...] = (value_total[...] + extra.reshape(nodes, rows, width)).astype(BF16)
    gh[...] = gh_in[...]


def per_device(
    ny,
    hidden_states,
    upper_gradient,
    w_query,
    key_projection,
    value_projection,
    query_gain,
    key_norm_gain,
    readout,
    cached_prefix_keys,
    cached_prefix_values,
    prefix_lengths,
    parents,
    visits,
):
    nl, ng = lax.axis_size("leaf"), lax.axis_size("head")
    nodes, rows, width = cached_prefix_keys.shape
    tokens, feats = hidden_states.shape
    model = w_query.shape[0]
    blocks = nl // (2 * ny) + 1
    span = max(2 * ny * rows, tokens)
    half = tokens // 2
    cols = (GROUP + 2) * width
    inverse = np.asarray(
        ROPE_BASE ** (-2.0 * (np.arange(width) % (width // 2)) / width), np.float32
    ).reshape(1, width)
    smem = pl.BlockSpec(memory_space=pltpu.SMEM)
    vmem = pl.BlockSpec(memory_space=pltpu.VMEM)
    anywhere = pl.BlockSpec(memory_space=pl.ANY)
    dma = pltpu.SemaphoreType.DMA
    rows_of_all = pltpu.VMEM((nl, rows, width), BF16)
    scratch = [
        pltpu.VMEM((model, cols), BF16),
        pltpu.VMEM((4, feats, cols), BF16),
        pltpu.VMEM((ng, tokens, feats), BF16),
        pltpu.VMEM((nodes, rows, width), BF16),
        pltpu.VMEM((nodes, rows, width), BF16),
        pltpu.VMEM((tokens, GROUP * width), BF16),
        pltpu.VMEM((GROUP, tokens, 2 * width), BF16),
        pltpu.VMEM((nl, 1, 128), jnp.int32),
        pltpu.SMEM((nl, 1, 128), jnp.int32),
        pltpu.VMEM((nl, 1, 128), F32),
        pltpu.VMEM((nl, 1, 128), F32),
        pltpu.VMEM((nl, 2, rows, width), BF16),
        pltpu.VMEM((nl, 2, rows, width), BF16),
        pltpu.VMEM((tokens, cols), F32),
        pltpu.VMEM((tokens, width), F32),
        pltpu.VMEM((tokens, width), F32),
        pltpu.VMEM((GROUP, tokens, width), BF16),
        pltpu.VMEM((2, tokens, width), BF16),
        pltpu.VMEM((blocks, GROUP, span, tokens), F32),
        pltpu.VMEM((blocks, GROUP, span, tokens), F32),
        pltpu.VMEM((blocks, span, 16), F32),
        pltpu.VMEM((GROUP, tokens), F32),
        pltpu.VMEM((GROUP, tokens), F32),
        pltpu.VMEM((GROUP, tokens), F32),
        pltpu.VMEM((blocks, GROUP, tokens), F32),
        pltpu.VMEM((blocks, span, 2 * width), F32),
        pltpu.VMEM((2, blocks, GROUP, span, tokens), BF16),
        pltpu.VMEM((ng, 1, 128), F32),
        pltpu.VMEM((nl, 2, 128), F32),
        pltpu.VMEM((nl, 2, 128), F32),
        rows_of_all,
        rows_of_all,
        rows_of_all,
        rows_of_all,
        pltpu.VMEM((GROUP + 2, 2, tokens, width), BF16),
        pltpu.VMEM((GROUP + 2, 2, tokens, width), BF16),
        pltpu.VMEM((2, tokens, cols), BF16),
        pltpu.VMEM((4, tokens, feats), F32),
        pltpu.VMEM((6, half, feats), BF16),
        pltpu.VMEM((6, half, feats), BF16),
        dma((7,)),
        dma,
        dma,
        dma,
        dma,
        dma((blocks - 1,)),
        dma((14,)),
        dma((ng, 2)),
        dma((4,)),
        dma((4,)),
        dma,
        dma,
        dma,
        dma,
        dma,
        dma,
        dma,
        dma,
        dma((GROUP + 2,)),
        dma((GROUP + 2,)),
        dma((6,)),
        dma((6,)),
    ]
    table = jax.ShapeDtypeStruct((nodes, rows, width), BF16)
    per_slot = jax.ShapeDtypeStruct((nl, rows, width), BF16)
    grad_hidden = jax.ShapeDtypeStruct((tokens, feats), BF16)
    gh, dk, dv, cw, par = pl.pallas_call(
        functools.partial(main_kernel, ny),
        out_shape=(
            grad_hidden,
            per_slot,
            per_slot,
            jax.ShapeDtypeStruct((nl, 1, 128), F32),
            jax.ShapeDtypeStruct((nl, 1, 128), jnp.int32),
        ),
        in_specs=[smem, smem, smem, vmem] + [anywhere] * 5 + [vmem] * 3 + [anywhere] * 2,
        out_specs=(vmem, vmem, vmem, vmem, vmem),
        scratch_shapes=scratch,
        compiler_params=pltpu.CompilerParams(
            collective_id=0, has_side_effects=True, vmem_limit_bytes=58 * 1024 * 1024
        ),
    )(
        parents,
        visits,
        prefix_lengths,
        jnp.asarray(inverse),
        hidden_states,
        upper_gradient,
        w_query,
        key_projection,
        value_projection,
        query_gain.reshape(1, width),
        key_norm_gain.reshape(1, width),
        readout,
        cached_prefix_keys,
        cached_prefix_values,
    )
    return pl.pallas_call(
        collect_kernel,
        out_shape=(grad_hidden, table, table),
        in_specs=[smem] + [vmem] * 5,
        out_specs=(vmem, vmem, vmem),
        scratch_shapes=[
            pltpu.VMEM((nodes, rows, width), F32),
            pltpu.VMEM((nodes, rows, width), F32),
            pltpu.VMEM((nodes, 1, 128), F32),
        ],
        compiler_params=pltpu.CompilerParams(vmem_limit_bytes=16 * 1024 * 1024),
    )(par, readout, dk, dv, cw, gh)


def solution(mesh):
    in_specs = (
        P("leaf", "head"),
        P("leaf", "head"),
        P(None, "head"),
        P(None, "head"),
        P(None, "head"),
        P(),
        P(),
        P("head"),
        P(None, "leaf", "head"),
        P(None, "leaf", "head"),
        P(),
        P("leaf"),
        P("leaf"),
    )
    out_specs = (P("leaf", "head"), P(None, "leaf", "head"), P(None, "leaf", "head"))
    ny = 4 if mesh.shape["leaf"] % 4 == 0 else 1
    return jax.shard_map(
        functools.partial(per_device, ny),
        mesh=mesh,
        in_specs=in_specs,
        out_specs=out_specs,
        check_vma=False,
    )
```

```python
import functools

import jax
import jax.numpy as jnp
import numpy as np
from jax import lax
from jax.experimental import pallas as pl
from jax.experimental.pallas import tpu as pltpu
from jax.sharding import PartitionSpec as P

HEAD_SIZE = 128
GROUP = 4
EPS = 1e-06
ROPE_BASE = 1000000.0
LOSS_SCALE = 8192.0
SCALE = HEAD_SIZE ** (-0.5)
TILE = 64
BF16 = jnp.bfloat16
F32 = jnp.float32


def dot_nn(a, b):
    return lax.dot_general(a, b, (((1,), (0,)), ((), ())), preferred_element_type=F32)


def dot_nt(a, b):
    return lax.dot_general(a, b, (((1,), (1,)), ((), ())), preferred_element_type=F32)


def dot_tn(a, b):
    return lax.dot_general(a, b, (((0,), (0,)), ((), ())), preferred_element_type=F32)


def slot_offsets(nz, ny):
    order = [0]
    for step in range(1, nz // 2 + 1):
        order.append(step)
        if len(order) < nz:
            order.append(-step)
    return [(dz, dy) for dz in order for dy in range(ny)]


def main_kernel(
    ny,
    parents,
    visits,
    lengths,
    freq_in,
    hid,
    upper,
    wq,
    wk,
    wv,
    qgain_in,
    kgain_in,
    readout_in,
    ck,
    cv,
    gh_out,
    dk_out,
    dv_out,
    cw_out,
    par_out,
    freq,
    qgain,
    kgain,
    readout,
    w,
    wsib,
    hf,
    cks,
    cvs,
    up,
    ue,
    own_parent,
    own_visits,
    par,
    par_slots,
    cw,
    gh,
    hot,
    seen,
    kvs,
    kvf,
    acc,
    cosb,
    sinb,
    q,
    own,
    e,
    uv,
    rv,
    lsum,
    asum,
    bsum,
    tops,
    dv,
    gl,
    sch,
    sls,
    scl,
    dvs,
    dvr,
    dks,
    dkr,
    gx,
    gxr,
    gg,
    ps,
    rs_s,
    rs_r,
    in_sem,
    par_send,
    par_recv,
    out_sem,
    kv_send,
    kv_recv,
    ag_send,
    ag_recv,
    ws_send,
    ws_recv,
    sch_send,
    sch_recv,
    scl_send,
    scl_recv,
    dv_send,
    dv_recv,
    dk_send,
    dk_recv,
    gx_send,
    gx_recv,
    rs_send,
    rs_recv,
):
    me_l = lax.axis_index("leaf")
    me_g = lax.axis_index("head")
    nl = lax.axis_size("leaf")
    ng = lax.axis_size("head")
    nz = nl // ny
    nx = ng // 2
    z, y = me_l // ny, me_l % ny
    x, core = me_g // 2, me_g % 2
    nodes, rows, width = ck.shape
    tokens, feats = hid.shape
    half = tokens // 2
    offsets = slot_offsets(nz, ny)
    place = {(dz % nz, dy): slot for slot, (dz, dy) in enumerate(offsets)}
    mirror = [place[(-dz % nz, -dy % ny)] for dz, dy in offsets]
    per = 2 * ny
    chunks = nl // per

    def chip(dx, other=False):
        side = 1 - core if other else core
        return ((x + dx + nx) % nx) * 2 + side

    def leaf_of(slot):
        dz, dy = offsets[slot]
        return ((z + dz + nz) % nz) * ny + (y + dy) % ny

    def remote(src, dst, send, recv, **target):
        return pltpu.make_async_remote_copy(
            src_ref=src,
            dst_ref=dst,
            send_sem=send,
            recv_sem=recv,
            device_id=target,
            device_id_type=pl.DeviceIdType.MESH,
        )

    barrier = pltpu.get_barrier_semaphore()
    for o in range(1, nl):
        pl.semaphore_signal(
            barrier, inc=1, device_id={"leaf": (me_l + o) % nl}, device_id_type=pl.DeviceIdType.MESH
        )
    for o in range(1, ng):
        pl.semaphore_signal(
            barrier, inc=1, device_id={"head": (me_g + o) % ng}, device_id_type=pl.DeviceIdType.MESH
        )
    loads = [
        pltpu.make_async_copy(hid, hf.at[me_g], in_sem.at[0]),
        pltpu.make_async_copy(ck, cks, in_sem.at[1]),
        pltpu.make_async_copy(cv, cvs, in_sem.at[2]),
        pltpu.make_async_copy(wq, w.at[:, pl.ds(0, GROUP * width)], in_sem.at[3]),
        pltpu.make_async_copy(wk, w.at[:, pl.ds(GROUP * width, width)], in_sem.at[4]),
        pltpu.make_async_copy(wv, w.at[:, pl.ds((GROUP + 1) * width, width)], in_sem.at[5]),
        pltpu.make_async_copy(upper, up, in_sem.at[6]),
    ]
    small_loads = [
        pltpu.make_async_copy(freq_in, freq, in_sem.at[9]),
        pltpu.make_async_copy(qgain_in, qgain, in_sem.at[10]),
        pltpu.make_async_copy(kgain_in, kgain, in_sem.at[11]),
        pltpu.make_async_copy(readout_in, readout, in_sem.at[12]),
    ]
    first_loads = [
        pltpu.make_async_copy(parents, own_parent, in_sem.at[7]),
        pltpu.make_async_copy(visits, own_visits, in_sem.at[8]),
    ]
    for load in first_loads + loads + small_loads:
        load.start()

    lane = lax.broadcasted_iota(jnp.int32, (1, 128), 1)
    for load in first_loads:
        load.wait()
    parent = own_parent[0]
    par[pl.ds(me_l, 1)] = jnp.where(lane == 0, parent, own_visits[0]).reshape(1, 1, 128)
    pl.semaphore_wait(barrier, nl - 1 + ng - 1)

    planes = [0] + [abs(dz) for dz, _ in offsets[ny::ny]]
    for slot in range(1, nl):
        remote(
            par.at[me_l],
            par.at[me_l],
            par_send,
            par_recv.at[planes[slot // ny]],
            leaf=leaf_of(slot),
        ).start()

    loads[0].wait()

    def ag_copy(sem, block, part, target):
        rows_at = hf.at[block, pl.ds(part * half, half)]
        return remote(rows_at, rows_at, ag_send.at[sem], ag_recv.at[block, part], head=target)

    def ag_wait(block, part):
        rows_at = hf.at[block, pl.ds(part * half, half)]
        remote(rows_at, rows_at, ag_send.at[0], ag_recv.at[block, part], head=me_g).wait_recv()

    right, left, sibling = chip(1), chip(-1), chip(0, True)
    ag = [
        ag_copy(0, me_g, 0, right),
        ag_copy(1, me_g, 1, left),
        ag_copy(2, me_g, 1, right),
        ag_copy(3, me_g, 0, left),
        ag_copy(4, me_g, 0, sibling),
        ag_copy(5, me_g, 1, sibling),
    ]
    for copy in ag:
        copy.start()

    loads[1].wait()
    loads[2].wait()
    for plane in range(nz // 2 + 1):
        members = [slot for slot in range(nl) if planes[slot // ny] == plane]
        some = par.at[pl.ds(0, len([slot for slot in members if slot > 0]))]
        remote(some, some, par_send, par_recv.at[plane], leaf=me_l).wait_recv()
        for slot in members:
            dest = leaf_of(mirror[slot])
            node = par[dest, 0, 0]
            if slot == 0:
                kvf[0, 0] = cks[node]
                kvf[0, 1] = cvs[node]
            else:
                kvs[slot, 0] = cks[node]
                kvs[slot, 1] = cvs[node]
                remote(
                    kvs.at[slot], kvf.at[slot], kv_send, kv_recv.at[slot // per], leaf=dest
                ).start()

    def pass_on(*copies):
        for copy in copies:
            copy.start()
            ag.append(copy)

    ag_wait(left, 0)
    pass_on(ag_copy(6, left, 0, right), ag_copy(7, left, 0, sibling))
    ag_wait(right, 1)
    pass_on(ag_copy(8, right, 1, left), ag_copy(9, right, 1, sibling))

    for slot in range(nl):
        src = leaf_of(slot)
        par_row = jnp.full((1, 128), par[src, 0, 0], jnp.int32)
        par_slots[slot] = par_row
        hot[slot] = jnp.where((lane == par_row) & (lane < nodes), 1.0, 0.0)
        seen[slot] = jnp.full((1, 128), par[src, 0, 1], jnp.int32).astype(F32)
    outs = [pltpu.make_async_copy(par_slots, par_out, out_sem.at[0])]
    outs[0].start()

    for load in small_loads:
        load.wait()
    length = lengths[parent]
    position = (length + lax.broadcasted_iota(jnp.int32, (tokens, width), 0)).astype(F32)
    angle = position * freq[...]
    cosb[...] = jnp.cos(angle)
    low = lax.broadcasted_iota(jnp.int32, (tokens, width), 1) < width // 2
    sine = jnp.sin(angle)
    sinb[...] = jnp.where(low, -sine, sine)

    def rotate(value):
        return value * cosb[...] + pltpu.roll(value, width // 2, 1) * sinb[...]

    def rotate_back(value):
        return value * cosb[...] - pltpu.roll(value, width // 2, 1) * sinb[...]

    loads[6].wait()
    at_lane = lax.broadcasted_iota(jnp.int32, (tokens, width), 1)
    for h in range(GROUP):
        ue[h, :, 0:width] = up[:, h * width : (h + 1) * width]
        ue[h, :, width : 2 * width] = jnp.where(at_lane == h, 1.0, 0.0).astype(BF16)
    read = [readout[h * width : (h + 1) * width].astype(F32).reshape(1, width) for h in range(GROUP)]
    read_rows = jnp.concatenate(read + [jnp.zeros((16 - GROUP, width), F32)], 0).astype(BF16)

    for i in (3, 4, 5):
        loads[i].wait()

    def block_rows(block):
        return pl.ds(pl.multiple_of(block * feats, feats), feats)

    def project(block, first=False):
        part = dot_nn(hf[block], w[block_rows(block), :])
        if first:
            acc[...] = part
        else:
            acc[...] += part

    def keys_of(i, which=0):
        if i == chunks:
            return own[which]
        return kvf[pl.ds(i * per, per), which].reshape(per * rows, width)

    def wait_rows(i):
        skip = 1 if i == 0 else 0
        some = kvf.at[pl.ds(i * per + skip, per - skip)]
        remote(some, some, kv_send, kv_recv.at[i], leaf=me_l).wait_recv()

    def values_product(i):
        values = keys_of(i, 1)
        for h in range(GROUP):
            uv[i, h] = dot_nt(values, up[:, h * width : (h + 1) * width])
        rv[i] = dot_nt(values, read_rows)

    project(me_g, True)

    ag_wait(sibling, 0)
    ag_wait(sibling, 1)
    project(sibling)
    ag_wait(left, 1)
    ag_wait(right, 0)
    pass_on(ag_copy(10, left, 1, sibling), ag_copy(11, right, 0, sibling))
    project(left)
    project(right)

    def project_other(dx):
        block = chip(dx, True)
        ag_wait(block, 0)
        ag_wait(block, 1)
        project(block)

    project_other(-1)
    project_other(1)
    wait_rows(0)
    values_product(0)
    opposite = chip(2)
    ag_wait(opposite, 0)
    pass_on(ag_copy(12, opposite, 0, sibling))
    ag_wait(opposite, 1)
    pass_on(ag_copy(13, opposite, 1, sibling))
    project(opposite)
    project_other(2)

    hops = (2, 1, -1, 0)
    ws_copies = []
    for j, dx in enumerate(hops):
        copy = remote(
            w.at[block_rows(chip(dx, True))], wsib.at[j], ws_send.at[j], ws_recv.at[j], head=sibling
        )
        copy.start()
        ws_copies.append(copy)

    def norm_inverse(raw):
        return lax.rsqrt(jnp.mean(raw * raw, axis=-1, keepdims=True) + EPS)

    for h in range(GROUP + 1):
        raw = acc[:, h * width : (h + 1) * width]
        gain = qgain[...] if h < GROUP else kgain[...]
        turned = rotate(raw * norm_inverse(raw) * gain).astype(BF16)
        if h < GROUP:
            q[h] = turned
        else:
            own[0] = turned
    own[1] = acc[:, (GROUP + 1) * width :].astype(BF16)

    def forward(i, first):
        keys = keys_of(i)
        if i == chunks:
            shape = (tokens, tokens)
            mask = lax.broadcasted_iota(jnp.int32, shape, 0) <= lax.broadcasted_iota(
                jnp.int32, shape, 1
            )
        else:
            at = lax.broadcasted_iota(jnp.int32, (rows, tokens), 0)
            mask = (
                jnp.concatenate([at + leaf_of(i * per + b) * rows for b in range(per)], 0) < length
            )
        for h in range(GROUP):
            logits = jnp.where(mask, dot_nt(keys, q[h]) * SCALE, -1e30)
            top = jnp.max(logits, axis=0, keepdims=True)
            if not first:
                before = tops[i_last[0], h : h + 1, :]
                top = jnp.maximum(top, before)
            weight = jnp.exp(logits - top)
            total = jnp.sum(weight, axis=0, keepdims=True)
            a = jnp.sum(weight * rv[i][:, h : h + 1], axis=0, keepdims=True)
            if not first:
                fade = jnp.exp(before - top)
                total += lsum[h : h + 1, :] * fade
                a += asum[h : h + 1, :] * fade
            lsum[h : h + 1, :] = total
            asum[h : h + 1, :] = a
            tops[i, h : h + 1, :] = top
            e[i, h] = weight
        i_last[0] = i

    i_last = [None]
    values_product(chunks)
    forward(chunks, True)
    forward(0, False)
    for i in range(1, chunks):
        wait_rows(i)
        values_product(i)
        forward(i, False)

    score = jnp.zeros((1, 1), F32)
    for h in range(GROUP):
        inverse = 1.0 / lsum[h : h + 1, :]
        lsum[h : h + 1, :] = inverse
        a = asum[h : h + 1, :] * inverse
        asum[h : h + 1, :] = a
        score += jnp.sum(a, axis=1, keepdims=True)
    sch[0] = jnp.broadcast_to(score / tokens, (1, 128))
    for o in range(1, ng):
        remote(sch.at[0], sch.at[o], sch_send, sch_recv, head=(me_g + o) % ng).start()

    for h in range(GROUP):
        b = jnp.zeros((1, tokens), F32)
        for i in range(chunks + 1):
            factor = lsum[h : h + 1, :]
            if i != chunks - 1:
                factor *= jnp.exp(tops[i, h : h + 1, :] - tops[chunks - 1, h : h + 1, :])
            for at in range(0, keys_of(i).shape[0], TILE):
                tile = slice(at, at + TILE)
                prob = e[i, h, tile] * factor
                e[i, h, tile] = prob
                gl[0, i, h, tile] = prob.astype(BF16)
                b += jnp.sum(prob * uv[i, h, tile], axis=0, keepdims=True)
            term = dot_nn(gl[0, i, h], ue[h])
            if h == 0:
                dv[i] = term
            else:
                dv[i] += term
        bsum[h : h + 1, :] = b

    def send_rows(buffer, target, send, recv, slot):
        remote(buffer.at[slot], target.at[mirror[slot]], send, recv, leaf=leaf_of(slot)).start()

    def send_values(i):
        dvs[pl.ds(i * per, per)] = dv[i][:, :width].astype(BF16).reshape(per, rows, width)
        for slot in range(i * per, (i + 1) * per):
            if slot == 0:
                dvr[0] = dvs[0]
            else:
                send_rows(dvs, dvr, dv_send, dv_recv, slot)

    parts = 128 // rows
    group = lane // rows
    diagonal = lax.broadcasted_iota(jnp.int32, (8, 128), 0) == lax.broadcasted_iota(
        jnp.int32, (8, 128), 1
    ) // rows
    for i in range(chunks):
        sums = dv[i][:, width:].T[0:8]
        for j in range(per // parts):
            tile = sums[:, j * 128 : (j + 1) * 128]
            turns = []
            for k in range(parts):
                moved = tile if k == 0 else pltpu.roll(tile, rows * k, 1)
                turns.append(jnp.sum(jnp.where(diagonal, moved, 0.0), axis=0, keepdims=True))
            for b in range(parts):
                line = turns[(0 - b) % parts]
                for h in range(1, parts):
                    line = jnp.where(group == h, turns[(h - b) % parts], line)
                sls[i * per + j * parts + b, 1:2] = line

    def norm_back(raw, gain, grad):
        inverse = norm_inverse(raw)
        scaled = grad * gain
        mean = jnp.mean(raw * scaled, axis=-1, keepdims=True)
        return (inverse * scaled - raw * (inverse * inverse * inverse) * mean).astype(BF16)

    gx_copies = [
        remote(gx.at[j], gxr.at[j], gx_send.at[j], gx_recv.at[j], head=sibling)
        for j in range(GROUP + 2)
    ]

    def query_grads(h):
        back = [None, None]
        for i in range(chunks + 1):
            keys = keys_of(i)
            for at in range(0, keys.shape[0], TILE):
                tile = slice(at, at + TILE)
                prob = e[i, h, tile] * SCALE
                grad = prob * (uv[i, h, tile] - bsum[h : h + 1, :])
                gl[0, i, h, tile] = grad.astype(BF16)
                grad = prob * (rv[i, tile, h : h + 1] - asum[h : h + 1, :])
                gl[1, i, h, tile] = grad.astype(BF16)
            for part in range(2):
                term = dot_tn(keys, gl[part, i, h])
                back[part] = term if i == 0 else back[part] + term
        raw = acc[:, h * width : (h + 1) * width]
        for part in range(2):
            gx[h, part] = norm_back(raw, qgain[...], rotate_back(back[part].T))
        gx_copies[h].start()

    query_grads(0)
    query_grads(1)

    some = sch.at[pl.ds(1, ng - 1)]
    remote(some, some, sch_send, sch_recv, head=me_g).wait_recv()
    step_score = jnp.sum(sch[...], axis=0)
    for slot in range(nl):
        sls[slot, 0:1] = step_score
    scl[0] = sls[0]
    for slot in range(1, nl):
        send_rows(sls, scl, scl_send, scl_recv, slot)
    for i in range(chunks):
        send_values(i)
    for h in range(2, GROUP):
        query_grads(h)

    read_value = None
    for h in range(GROUP):
        term = dv[chunks][:, width + h : width + h + 1] * read[h]
        read_value = term if read_value is None else read_value + term
    gx[GROUP + 1, 0] = dv[chunks][:, :width].astype(BF16)
    gx[GROUP + 1, 1] = read_value.astype(BF16)
    gx_copies[GROUP + 1].start()
    for part in range(2):
        back = None
        for h in range(GROUP):
            term = dot_nn(gl[part, chunks, h], q[h])
            back = term if back is None else back + term
        cols = slice(GROUP * width, (GROUP + 1) * width)
        gx[GROUP, part] = norm_back(acc[:, cols], kgain[...], rotate_back(back))
    gx_copies[GROUP].start()

    some = scl.at[pl.ds(1, nl - 1)]
    remote(some, some, scl_send, scl_recv, leaf=me_l).wait_recv()
    match = hot[...]
    grown = jnp.exp(scl[:, 0:1, :])
    count = seen[...]
    node_total = jnp.sum(match * grown, axis=0, keepdims=True)
    node_seen = jnp.sum(match * count, axis=0, keepdims=True)
    total = jnp.sum(match * node_total, axis=2, keepdims=True)
    total_seen = jnp.sum(match * node_seen, axis=2, keepdims=True)
    scales = (LOSS_SCALE / tokens) * (grown / total - count / total_seen)
    cw[...] = scales * scl[:, 1:2, :]
    outs.append(pltpu.make_async_copy(cw, cw_out, out_sem.at[1]))
    outs[1].start()
    scale = scales[0, :, 0:1]

    for j in range(GROUP + 2):
        cols = slice(j * width, (j + 1) * width)
        gg[0, :, cols] = (gx[j, 0].astype(F32) + scale * gx[j, 1].astype(F32)).astype(BF16)
    for j in range(GROUP + 2):
        cols = slice(j * width, (j + 1) * width)
        gx_copies[j].wait_recv()
        gg[1, :, cols] = (gxr[j, 0].astype(F32) + scale * gxr[j, 1].astype(F32)).astype(BF16)

    def term(j):
        ws_copies[j].wait_recv()
        ps[j] = dot_nt(gg[0], w[block_rows(chip(hops[j])), :]) + dot_nt(gg[1], wsib[j])

    rs_copies = []

    def rs_send_rows(value, target):
        slot = len(rs_copies)
        rs_s[slot] = value.astype(BF16)
        copy = remote(
            rs_s.at[slot], rs_r.at[slot], rs_send.at[slot], rs_recv.at[slot], head=target
        )
        copy.start()
        rs_copies.append(copy)

    first, second = slice(0, half), slice(half, tokens)
    term(0)
    rs_send_rows(ps[0, first], right)
    rs_send_rows(ps[0, second], left)

    def send_keys(i):
        total = None
        for h in range(GROUP):
            for at in range(0, per * rows, TILE):
                tile = slice(at, at + TILE)
                grad = gl[0, i, h, tile].astype(F32) + scale * gl[1, i, h, tile].astype(F32)
                gl[0, i, h, tile] = grad.astype(BF16)
            part = dot_nn(gl[0, i, h], q[h])
            total = part if total is None else total + part
        dks[pl.ds(i * per, per)] = total.astype(BF16).reshape(per, rows, width)
        for slot in range(i * per, (i + 1) * per):
            if slot == 0:
                dkr[0] = dks[0]
            else:
                send_rows(dks, dkr, dk_send, dk_recv, slot)

    for i in range(chunks // 2):
        send_keys(i)
    term(1)
    rs_send_rows(ps[1, second], right)
    term(2)
    rs_send_rows(ps[2, first], left)
    for i in range(chunks // 2, chunks):
        send_keys(i)
    rs_copies[0].wait_recv()
    rs_send_rows(ps[1, first] + rs_r[0].astype(F32), right)
    rs_copies[1].wait_recv()
    rs_send_rows(ps[2, second] + rs_r[1].astype(F32), left)
    term(3)

    some = dvr.at[pl.ds(1, nl - 1)]
    remote(some, some, dv_send, dv_recv, leaf=me_l).wait_recv()
    outs.append(pltpu.make_async_copy(dvr, dv_out, out_sem.at[2]))
    outs[2].start()
    remote(some, some, dk_send, dk_recv, leaf=me_l).wait_recv()
    outs.append(pltpu.make_async_copy(dkr, dk_out, out_sem.at[3]))
    outs[3].start()

    for slot in range(2, 6):
        rs_copies[slot].wait_recv()
    gh[first, :] = (ps[3, first] + rs_r[4].astype(F32) + rs_r[3].astype(F32)).astype(BF16)
    gh[second, :] = (ps[3, second] + rs_r[2].astype(F32) + rs_r[5].astype(F32)).astype(BF16)

    outs.append(pltpu.make_async_copy(gh, gh_out, out_sem.at[4]))
    outs[4].start()

    for copy in ag + ws_copies + gx_copies + rs_copies:
        copy.wait_send()
    for buffer, send, recv in (
        (par, par_send, par_recv),
        (kvs, kv_send, kv_recv.at[0]),
        (dvs, dv_send, dv_recv),
        (dks, dk_send, dk_recv),
        (sls, scl_send, scl_recv),
    ):
        some = buffer.at[pl.ds(0, nl - 1)]
        remote(some, some, send, recv, leaf=me_l).wait_send()
    some = sch.at[pl.ds(1, ng - 1)]
    remote(some, some, sch_send, sch_recv, head=me_g).wait_send()
    for out in outs:
        out.wait()


def collect_kernel(par, readout, cw, dk_in, dv_in, gh_in, gh, gk, gv, key_total, value_total, sums):
    nodes, rows, width = gk.shape
    key_total[...] = jnp.zeros_like(key_total)
    value_total[...] = jnp.zeros_like(value_total)
    sums[...] = jnp.zeros_like(sums)

    def add(s, c):
        node = par[s, 0, 0]
        key_total[node] += dk_in[s].astype(F32)
        value_total[node] += dv_in[s].astype(F32)
        sums[node] += cw[s]
        return c

    lax.fori_loop(0, dk_in.shape[0], add, 0, unroll=4)
    gk[...] = key_total[...].astype(BF16)
    shape = (1, rows, 128)
    keep = lax.broadcasted_iota(jnp.int32, shape, 2) % rows == lax.broadcasted_iota(
        jnp.int32, shape, 1
    )
    left = jnp.where(keep, sums[...], 0.0).reshape(nodes * rows, 128)
    high = left.astype(BF16)
    rest = (left - high.astype(F32)).astype(BF16)
    right = jnp.concatenate(
        [
            jnp.broadcast_to(
                readout[h * width : (h + 1) * width].astype(F32).reshape(1, width), (rows, width)
            )
            for h in range(128 // rows)
        ],
        0,
    ).astype(BF16)
    extra = dot_nn(high, right) + dot_nn(rest, right)
    gv[...] = (value_total[...] + extra.reshape(nodes, rows, width)).astype(BF16)
    gh[...] = gh_in[...]


def per_device(
    ny,
    hidden_states,
    upper_gradient,
    w_query,
    key_projection,
    value_projection,
    query_gain,
    key_norm_gain,
    readout,
    cached_prefix_keys,
    cached_prefix_values,
    prefix_lengths,
    parents,
    visits,
):
    nl, ng = lax.axis_size("leaf"), lax.axis_size("head")
    nodes, rows, width = cached_prefix_keys.shape
    tokens, feats = hidden_states.shape
    model = w_query.shape[0]
    blocks = nl // (2 * ny) + 1
    span = max(2 * ny * rows, tokens)
    half = tokens // 2
    cols = (GROUP + 2) * width
    inverse = np.asarray(
        ROPE_BASE ** (-2.0 * (np.arange(width) % (width // 2)) / width), np.float32
    ).reshape(1, width)
    smem = pl.BlockSpec(memory_space=pltpu.SMEM)
    vmem = pl.BlockSpec(memory_space=pltpu.VMEM)
    anywhere = pl.BlockSpec(memory_space=pl.ANY)
    hbm = pl.BlockSpec(memory_space=pltpu.HBM)
    dma = pltpu.SemaphoreType.DMA
    rows_of_all = pltpu.VMEM((nl, rows, width), BF16)
    scratch = [
        pltpu.VMEM((1, width), F32),
        pltpu.VMEM((1, width), F32),
        pltpu.VMEM((1, width), F32),
        pltpu.VMEM((GROUP * width,), BF16),
        pltpu.VMEM((model, cols), BF16),
        pltpu.VMEM((4, feats, cols), BF16),
        pltpu.VMEM((ng, tokens, feats), BF16),
        pltpu.VMEM((nodes, rows, width), BF16),
        pltpu.VMEM((nodes, rows, width), BF16),
        pltpu.VMEM((tokens, GROUP * width), BF16),
        pltpu.VMEM((GROUP, tokens, 2 * width), BF16),
        pltpu.VMEM((1,), jnp.int32),
        pltpu.VMEM((1,), jnp.int32),
        pltpu.VMEM((nl, 1, 128), jnp.int32),
        pltpu.VMEM((nl, 1, 128), jnp.int32),
        pltpu.VMEM((nl, 1, 128), F32),
        pltpu.VMEM((tokens, feats), BF16),
        pltpu.VMEM((nl, 1, 128), F32),
        pltpu.VMEM((nl, 1, 128), F32),
        pltpu.VMEM((nl, 2, rows, width), BF16),
        pltpu.VMEM((nl, 2, rows, width), BF16),
        pltpu.VMEM((tokens, cols), F32),
        pltpu.VMEM((tokens, width), F32),
        pltpu.VMEM((tokens, width), F32),
        pltpu.VMEM((GROUP, tokens, width), BF16),
        pltpu.VMEM((2, tokens, width), BF16),
        pltpu.VMEM((blocks, GROUP, span, tokens), F32),
        pltpu.VMEM((blocks, GROUP, span, tokens), F32),
        pltpu.VMEM((blocks, span, 16), F32),
        pltpu.VMEM((GROUP, tokens), F32),
        pltpu.VMEM((GROUP, tokens), F32),
        pltpu.VMEM((GROUP, tokens), F32),
        pltpu.VMEM((blocks, GROUP, tokens), F32),
        pltpu.VMEM((blocks, span, 2 * width), F32),
        pltpu.VMEM((2, blocks, GROUP, span, tokens), BF16),
        pltpu.VMEM((ng, 1, 128), F32),
        pltpu.VMEM((nl, 2, 128), F32),
        pltpu.VMEM((nl, 2, 128), F32),
        rows_of_all,
        rows_of_all,
        rows_of_all,
        rows_of_all,
        pltpu.VMEM((GROUP + 2, 2, tokens, width), BF16),
        pltpu.VMEM((GROUP + 2, 2, tokens, width), BF16),
        pltpu.VMEM((2, tokens, cols), BF16),
        pltpu.VMEM((4, tokens, feats), F32),
        pltpu.VMEM((6, half, feats), BF16),
        pltpu.VMEM((6, half, feats), BF16),
        dma((13,)),
        dma,
        dma((blocks,)),
        dma((5,)),
        dma,
        dma((blocks - 1,)),
        dma((14,)),
        dma((ng, 2)),
        dma((4,)),
        dma((4,)),
        dma,
        dma,
        dma,
        dma,
        dma,
        dma,
        dma,
        dma,
        dma((GROUP + 2,)),
        dma((GROUP + 2,)),
        dma((6,)),
        dma((6,)),
    ]
    table = jax.ShapeDtypeStruct((nodes, rows, width), BF16)
    per_slot = jax.ShapeDtypeStruct((nl, rows, width), BF16)
    grad_hidden = jax.ShapeDtypeStruct((tokens, feats), BF16)
    gh, dk, dv, cw, par = pl.pallas_call(
        functools.partial(main_kernel, ny),
        out_shape=(
            grad_hidden,
            per_slot,
            per_slot,
            jax.ShapeDtypeStruct((nl, 1, 128), F32),
            jax.ShapeDtypeStruct((nl, 1, 128), jnp.int32),
        ),
        in_specs=[hbm, hbm, smem, hbm] + [anywhere] * 5 + [hbm] * 3 + [anywhere] * 2,
        out_specs=(anywhere,) * 5,
        scratch_shapes=scratch,
        compiler_params=pltpu.CompilerParams(
            collective_id=0, has_side_effects=True, vmem_limit_bytes=58 * 1024 * 1024
        ),
    )(
        parents,
        visits,
        prefix_lengths,
        jnp.asarray(inverse),
        hidden_states,
        upper_gradient,
        w_query,
        key_projection,
        value_projection,
        query_gain.reshape(1, width),
        key_norm_gain.reshape(1, width),
        readout,
        cached_prefix_keys,
        cached_prefix_values,
    )
    return pl.pallas_call(
        collect_kernel,
        out_shape=(grad_hidden, table, table),
        in_specs=[smem] + [vmem] * 5,
        out_specs=(vmem,) * 3,
        scratch_shapes=[
            pltpu.VMEM((nodes, rows, width), F32),
            pltpu.VMEM((nodes, rows, width), F32),
            pltpu.VMEM((nodes, 1, 128), F32),
        ],
        compiler_params=pltpu.CompilerParams(vmem_limit_bytes=58 * 1024 * 1024),
    )(par, readout, cw, dk, dv, gh)


def solution(mesh):
    in_specs = (
        P("leaf", "head"),
        P("leaf", "head"),
        P(None, "head"),
        P(None, "head"),
        P(None, "head"),
        P(),
        P(),
        P("head"),
        P(None, "leaf", "head"),
        P(None, "leaf", "head"),
        P(),
        P("leaf"),
        P("leaf"),
    )
    out_specs = (P("leaf", "head"), P(None, "leaf", "head"), P(None, "leaf", "head"))
    ny = 4 if mesh.shape["leaf"] % 4 == 0 else 1
    return jax.shard_map(
        functools.partial(per_device, ny),
        mesh=mesh,
        in_specs=in_specs,
        out_specs=out_specs,
        check_vma=False,
    )
```

```python
import functools

import jax
import jax.numpy as jnp
import numpy as np
from jax import lax
from jax.experimental import pallas as pl
from jax.experimental.pallas import tpu as pltpu
from jax.sharding import PartitionSpec as P

HEAD_SIZE = 128
GROUP = 4
EPS = 1e-06
ROPE_BASE = 1000000.0
LOSS_SCALE = 8192.0
SCALE = HEAD_SIZE ** (-0.5)
TILE = 64
BF16 = jnp.bfloat16
F32 = jnp.float32


def dot_nn(a, b):
    return lax.dot_general(a, b, (((1,), (0,)), ((), ())), preferred_element_type=F32)


def dot_nt(a, b):
    return lax.dot_general(a, b, (((1,), (1,)), ((), ())), preferred_element_type=F32)


def dot_tn(a, b):
    return lax.dot_general(a, b, (((0,), (0,)), ((), ())), preferred_element_type=F32)


def slot_offsets(nz, ny):
    order = [0]
    for step in range(1, nz // 2 + 1):
        order.append(step)
        if len(order) < nz:
            order.append(-step)
    return [(dz, dy) for dz in order for dy in range(ny)]


def main_kernel(
    ny,
    parents,
    visits,
    lengths,
    freq_in,
    hid,
    upper,
    wq,
    wk,
    wv,
    qgain_in,
    kgain_in,
    readout_in,
    ck,
    cv,
    gh_out,
    dk_out,
    dv_out,
    cw_out,
    par_out,
    freq,
    qgain,
    kgain,
    readout,
    w,
    wsib,
    hf,
    cks,
    cvs,
    up,
    ue,
    own_parent,
    own_visits,
    par,
    par_slots,
    cw,
    gh,
    hot,
    seen,
    kvs,
    kvf,
    acc,
    cosb,
    sinb,
    q,
    own,
    e,
    uv,
    rv,
    lsum,
    asum,
    bsum,
    tops,
    dv,
    gl,
    dk,
    sch,
    sls,
    scl,
    dvs,
    dvr,
    dks,
    dkr,
    gx,
    gxr,
    gab,
    gg,
    far,
    ps,
    rs_s,
    rs_r,
    in_sem,
    par_send,
    par_recv,
    out_sem,
    kv_send,
    kv_recv,
    ag_send,
    ag_recv,
    ws_send,
    ws_recv,
    sch_send,
    sch_recv,
    scl_send,
    scl_recv,
    dv_send,
    dv_recv,
    dk_send,
    dk_recv,
    gx_send,
    gx_recv,
    rs_send,
    rs_recv,
):
    me_l = lax.axis_index("leaf")
    me_g = lax.axis_index("head")
    nl = lax.axis_size("leaf")
    ng = lax.axis_size("head")
    nz = nl // ny
    nx = ng // 2
    z, y = me_l // ny, me_l % ny
    x, core = me_g // 2, me_g % 2
    nodes, rows, width = ck.shape
    tokens, feats = hid.shape
    half = tokens // 2
    offsets = slot_offsets(nz, ny)
    place = {(dz % nz, dy): slot for slot, (dz, dy) in enumerate(offsets)}
    mirror = [place[(-dz % nz, -dy % ny)] for dz, dy in offsets]
    per = 2 * ny
    chunks = nl // per

    def chip(dx, other=False):
        side = 1 - core if other else core
        return ((x + dx + nx) % nx) * 2 + side

    def leaf_of(slot):
        dz, dy = offsets[slot]
        return ((z + dz + nz) % nz) * ny + (y + dy) % ny

    def remote(src, dst, send, recv, **target):
        return pltpu.make_async_remote_copy(
            src_ref=src,
            dst_ref=dst,
            send_sem=send,
            recv_sem=recv,
            device_id=target,
            device_id_type=pl.DeviceIdType.MESH,
        )

    barrier = pltpu.get_barrier_semaphore()
    for o in range(1, nl):
        pl.semaphore_signal(
            barrier, inc=1, device_id={"leaf": (me_l + o) % nl}, device_id_type=pl.DeviceIdType.MESH
        )
    for o in range(1, ng):
        pl.semaphore_signal(
            barrier, inc=1, device_id={"head": (me_g + o) % ng}, device_id_type=pl.DeviceIdType.MESH
        )
    loads = [
        pltpu.make_async_copy(hid, hf.at[me_g], in_sem.at[0]),
        pltpu.make_async_copy(ck, cks, in_sem.at[1]),
        pltpu.make_async_copy(cv, cvs, in_sem.at[2]),
        pltpu.make_async_copy(wq, w.at[:, pl.ds(0, GROUP * width)], in_sem.at[3]),
        pltpu.make_async_copy(wk, w.at[:, pl.ds(GROUP * width, width)], in_sem.at[4]),
        pltpu.make_async_copy(wv, w.at[:, pl.ds((GROUP + 1) * width, width)], in_sem.at[5]),
        pltpu.make_async_copy(upper, up, in_sem.at[6]),
    ]
    small_loads = [
        pltpu.make_async_copy(freq_in, freq, in_sem.at[9]),
        pltpu.make_async_copy(qgain_in, qgain, in_sem.at[10]),
        pltpu.make_async_copy(kgain_in, kgain, in_sem.at[11]),
        pltpu.make_async_copy(readout_in, readout, in_sem.at[12]),
    ]
    first_loads = [
        pltpu.make_async_copy(parents, own_parent, in_sem.at[7]),
        pltpu.make_async_copy(visits, own_visits, in_sem.at[8]),
    ]
    for load in first_loads + loads + small_loads:
        load.start()

    lane = lax.broadcasted_iota(jnp.int32, (1, 128), 1)
    for load in first_loads:
        load.wait()
    parent = own_parent[0]
    par[pl.ds(me_l, 1)] = jnp.where(lane == 0, parent, own_visits[0]).reshape(1, 1, 128)
    pl.semaphore_wait(barrier, nl - 1 + ng - 1)

    planes = [0] + [abs(dz) for dz, _ in offsets[ny::ny]]
    for slot in range(1, nl):
        remote(
            par.at[me_l],
            par.at[me_l],
            par_send,
            par_recv.at[planes[slot // ny]],
            leaf=leaf_of(slot),
        ).start()

    loads[0].wait()

    def ag_copy(sem, block, part, target):
        rows_at = hf.at[block, pl.ds(part * half, half)]
        return remote(rows_at, rows_at, ag_send.at[sem], ag_recv.at[block, part], head=target)

    def ag_wait(block, part):
        rows_at = hf.at[block, pl.ds(part * half, half)]
        remote(rows_at, rows_at, ag_send.at[0], ag_recv.at[block, part], head=me_g).wait_recv()

    right, left, sibling = chip(1), chip(-1), chip(0, True)
    ag = [
        ag_copy(0, me_g, 0, right),
        ag_copy(1, me_g, 1, left),
        ag_copy(2, me_g, 1, right),
        ag_copy(3, me_g, 0, left),
        ag_copy(4, me_g, 0, sibling),
        ag_copy(5, me_g, 1, sibling),
    ]
    for copy in ag:
        copy.start()

    loads[1].wait()
    loads[2].wait()
    for plane in range(nz // 2 + 1):
        members = [slot for slot in range(nl) if planes[slot // ny] == plane]
        some = par.at[pl.ds(0, len([slot for slot in members if slot > 0]))]
        remote(some, some, par_send, par_recv.at[plane], leaf=me_l).wait_recv()
        for slot in members:
            dest = leaf_of(mirror[slot])
            node = par[dest, 0, 0]
            if slot == 0:
                kvf[0, 0] = cks[node]
                kvf[0, 1] = cvs[node]
            else:
                kvs[slot, 0] = cks[node]
                kvs[slot, 1] = cvs[node]
                remote(
                    kvs.at[slot], kvf.at[slot], kv_send, kv_recv.at[slot // per], leaf=dest
                ).start()

    def pass_on(*copies):
        for copy in copies:
            copy.start()
            ag.append(copy)

    ag_wait(left, 0)
    pass_on(ag_copy(6, left, 0, right), ag_copy(7, left, 0, sibling))
    ag_wait(right, 1)
    pass_on(ag_copy(8, right, 1, left), ag_copy(9, right, 1, sibling))

    for slot in range(nl):
        src = leaf_of(slot)
        par_row = jnp.full((1, 128), par[src, 0, 0], jnp.int32)
        par_slots[slot] = par_row
        hot[slot] = jnp.where((lane == par_row) & (lane < nodes), 1.0, 0.0)
        seen[slot] = jnp.full((1, 128), par[src, 0, 1], jnp.int32).astype(F32)
    outs = [pltpu.make_async_copy(par_slots, par_out, out_sem.at[0])]
    outs[0].start()

    for load in small_loads:
        load.wait()
    length = lengths[parent]
    position = (length + lax.broadcasted_iota(jnp.int32, (tokens, width), 0)).astype(F32)
    angle = position * freq[...]
    cosb[...] = jnp.cos(angle)
    low = lax.broadcasted_iota(jnp.int32, (tokens, width), 1) < width // 2
    sine = jnp.sin(angle)
    sinb[...] = jnp.where(low, -sine, sine)

    def rotate(value):
        return value * cosb[...] + pltpu.roll(value, width // 2, 1) * sinb[...]

    def rotate_back(value):
        return value * cosb[...] - pltpu.roll(value, width // 2, 1) * sinb[...]

    loads[6].wait()
    at_lane = lax.broadcasted_iota(jnp.int32, (tokens, width), 1)
    for h in range(GROUP):
        ue[h, :, 0:width] = up[:, h * width : (h + 1) * width]
        ue[h, :, width : 2 * width] = jnp.where(at_lane == h, 1.0, 0.0).astype(BF16)
    read = [readout[h * width : (h + 1) * width].astype(F32).reshape(1, width) for h in range(GROUP)]
    read_rows = jnp.concatenate(read + [jnp.zeros((16 - GROUP, width), F32)], 0).astype(BF16)

    for i in (3, 4, 5):
        loads[i].wait()

    def block_rows(block):
        return pl.ds(pl.multiple_of(block * feats, feats), feats)

    def project(block, first=False):
        part = dot_nn(hf[block], w[block_rows(block), :])
        if first:
            acc[...] = part
        else:
            acc[...] += part

    def keys_of(i, which=0):
        if i == chunks:
            return own[which]
        return kvf[pl.ds(i * per, per), which].reshape(per * rows, width)

    def wait_rows(i):
        skip = 1 if i == 0 else 0
        some = kvf.at[pl.ds(i * per + skip, per - skip)]
        remote(some, some, kv_send, kv_recv.at[i], leaf=me_l).wait_recv()

    def values_product(i):
        values = keys_of(i, 1)
        for h in range(GROUP):
            uv[i, h] = dot_nt(values, up[:, h * width : (h + 1) * width])
        rv[i] = dot_nt(values, read_rows)

    project(me_g, True)

    ag_wait(sibling, 0)
    ag_wait(sibling, 1)
    project(sibling)
    ag_wait(left, 1)
    ag_wait(right, 0)
    pass_on(ag_copy(10, left, 1, sibling), ag_copy(11, right, 0, sibling))
    project(left)
    project(right)

    def project_other(dx):
        block = chip(dx, True)
        ag_wait(block, 0)
        ag_wait(block, 1)
        project(block)

    project_other(-1)
    project_other(1)
    wait_rows(0)
    values_product(0)
    opposite = chip(2)
    ag_wait(opposite, 0)
    pass_on(ag_copy(12, opposite, 0, sibling))
    ag_wait(opposite, 1)
    pass_on(ag_copy(13, opposite, 1, sibling))
    project(opposite)
    project_other(2)

    hops = (2, 1, -1, 0)
    ws_copies = []
    for j, dx in enumerate(hops):
        copy = remote(
            w.at[block_rows(chip(dx, True))], wsib.at[j], ws_send.at[j], ws_recv.at[j], head=sibling
        )
        copy.start()
        ws_copies.append(copy)

    def norm_inverse(raw):
        return lax.rsqrt(jnp.mean(raw * raw, axis=-1, keepdims=True) + EPS)

    for h in range(GROUP + 1):
        raw = acc[:, h * width : (h + 1) * width]
        gain = qgain[...] if h < GROUP else kgain[...]
        turned = rotate(raw * norm_inverse(raw) * gain).astype(BF16)
        if h < GROUP:
            q[h] = turned
        else:
            own[0] = turned
    own[1] = acc[:, (GROUP + 1) * width :].astype(BF16)

    def forward(i, first):
        keys = keys_of(i)
        if i == chunks:
            shape = (tokens, tokens)
            mask = lax.broadcasted_iota(jnp.int32, shape, 0) <= lax.broadcasted_iota(
                jnp.int32, shape, 1
            )
        else:
            at = lax.broadcasted_iota(jnp.int32, (rows, tokens), 0)
            mask = (
                jnp.concatenate([at + leaf_of(i * per + b) * rows for b in range(per)], 0) < length
            )
        for h in range(GROUP):
            logits = jnp.where(mask, dot_nt(keys, q[h]) * SCALE, -1e30)
            top = jnp.max(logits, axis=0, keepdims=True)
            if not first:
                before = tops[i_last[0], h : h + 1, :]
                top = jnp.maximum(top, before)
            weight = jnp.exp(logits - top)
            total = jnp.sum(weight, axis=0, keepdims=True)
            a = jnp.sum(weight * rv[i][:, h : h + 1], axis=0, keepdims=True)
            if not first:
                fade = jnp.exp(before - top)
                total += lsum[h : h + 1, :] * fade
                a += asum[h : h + 1, :] * fade
            lsum[h : h + 1, :] = total
            asum[h : h + 1, :] = a
            tops[i, h : h + 1, :] = top
            e[i, h] = weight
        i_last[0] = i

    i_last = [None]
    values_product(chunks)
    forward(chunks, True)
    forward(0, False)
    for i in range(1, chunks):
        wait_rows(i)
        values_product(i)
        forward(i, False)

    score = jnp.zeros((1, 1), F32)
    for h in range(GROUP):
        inverse = 1.0 / lsum[h : h + 1, :]
        lsum[h : h + 1, :] = inverse
        a = asum[h : h + 1, :] * inverse
        asum[h : h + 1, :] = a
        score += jnp.sum(a, axis=1, keepdims=True)
    sch[0] = jnp.broadcast_to(score / tokens, (1, 128))
    for o in range(1, ng):
        remote(sch.at[0], sch.at[o], sch_send, sch_recv, head=(me_g + o) % ng).start()

    for h in range(GROUP):
        b = jnp.zeros((1, tokens), F32)
        for i in range(chunks + 1):
            factor = lsum[h : h + 1, :]
            if i != chunks - 1:
                factor *= jnp.exp(tops[i, h : h + 1, :] - tops[chunks - 1, h : h + 1, :])
            for at in range(0, keys_of(i).shape[0], TILE):
                tile = slice(at, at + TILE)
                prob = e[i, h, tile] * factor
                e[i, h, tile] = prob
                gl[0, i, h, tile] = prob.astype(BF16)
                b += jnp.sum(prob * uv[i, h, tile], axis=0, keepdims=True)
            term = dot_nn(gl[0, i, h], ue[h])
            if h == 0:
                dv[i] = term
            else:
                dv[i] += term
        bsum[h : h + 1, :] = b

    def send_rows(buffer, target, send, recv, slot):
        remote(buffer.at[slot], target.at[mirror[slot]], send, recv, leaf=leaf_of(slot)).start()

    def send_values(i):
        dvs[pl.ds(i * per, per)] = dv[i][:, :width].astype(BF16).reshape(per, rows, width)
        for slot in range(i * per, (i + 1) * per):
            if slot == 0:
                dvr[0] = dvs[0]
            else:
                send_rows(dvs, dvr, dv_send, dv_recv, slot)

    parts = 128 // rows
    group = lane // rows
    diagonal = lax.broadcasted_iota(jnp.int32, (8, 128), 0) == lax.broadcasted_iota(
        jnp.int32, (8, 128), 1
    ) // rows
    for i in range(chunks):
        sums = dv[i][:, width:].T[0:8]
        for j in range(per // parts):
            tile = sums[:, j * 128 : (j + 1) * 128]
            turns = []
            for k in range(parts):
                moved = tile if k == 0 else pltpu.roll(tile, rows * k, 1)
                turns.append(jnp.sum(jnp.where(diagonal, moved, 0.0), axis=0, keepdims=True))
            for b in range(parts):
                line = turns[(0 - b) % parts]
                for h in range(1, parts):
                    line = jnp.where(group == h, turns[(h - b) % parts], line)
                sls[i * per + j * parts + b, 1:2] = line

    def norm_back(raw, gain, grad):
        inverse = norm_inverse(raw)
        scaled = grad * gain
        mean = jnp.mean(raw * scaled, axis=-1, keepdims=True)
        return (inverse * scaled - raw * (inverse * inverse * inverse) * mean).astype(BF16)

    gx_copies = [
        remote(gx.at[j], gxr.at[j], gx_send.at[j], gx_recv.at[j], head=sibling)
        for j in range(GROUP + 2)
    ]

    def query_grads(h):
        back = [None, None]
        for i in range(chunks + 1):
            keys = keys_of(i)
            for at in range(0, keys.shape[0], TILE):
                tile = slice(at, at + TILE)
                prob = e[i, h, tile] * SCALE
                grad = prob * (uv[i, h, tile] - bsum[h : h + 1, :])
                gl[0, i, h, tile] = grad.astype(BF16)
                grad = prob * (rv[i, tile, h : h + 1] - asum[h : h + 1, :])
                gl[1, i, h, tile] = grad.astype(BF16)
            for part in range(2):
                term = dot_tn(keys, gl[part, i, h])
                back[part] = term if i == 0 else back[part] + term
        raw = acc[:, h * width : (h + 1) * width]
        for part in range(2):
            gx[h, part] = norm_back(raw, qgain[...], rotate_back(back[part].T))
        gx_copies[h].start()

    query_grads(0)
    query_grads(1)

    some = sch.at[pl.ds(1, ng - 1)]
    remote(some, some, sch_send, sch_recv, head=me_g).wait_recv()
    step_score = jnp.sum(sch[...], axis=0)
    for slot in range(nl):
        sls[slot, 0:1] = step_score
    scl[0] = sls[0]
    for slot in range(1, nl):
        send_rows(sls, scl, scl_send, scl_recv, slot)
    for i in range(1):
        send_values(i)
    query_grads(2)
    for i in range(1,4):
        send_values(i)
    query_grads(3)

    read_value = None
    for h in range(GROUP):
        term = dv[chunks][:, width + h : width + h + 1] * read[h]
        read_value = term if read_value is None else read_value + term
    gx[GROUP + 1, 0] = dv[chunks][:, :width].astype(BF16)
    gx[GROUP + 1, 1] = read_value.astype(BF16)
    gx_copies[GROUP + 1].start()
    for part in range(2):
        back = None
        for h in range(GROUP):
            term = dot_nn(gl[part, chunks, h], q[h])
            back = term if back is None else back + term
        cols = slice(GROUP * width, (GROUP + 1) * width)
        gx[GROUP, part] = norm_back(acc[:, cols], kgain[...], rotate_back(back))
    gx_copies[GROUP].start()

    for i in range(chunks):
        for part in range(2):
            total = None
            for h in range(GROUP):
                product = dot_nn(gl[part, i, h], q[h])
                total = product if total is None else total + product
            dk[part, i] = total
    for j in range(GROUP + 2):
        cols = slice(j * width, (j + 1) * width)
        gx_copies[j].wait_recv()
        for part in range(2):
            gab[0, part, :, cols] = gx[j, part]
            gab[1, part, :, cols] = gxr[j, part]

    def term(left, j):
        return dot_nt(left[0], w[block_rows(chip(hops[j])), :]) + dot_nt(left[1], wsib[j])

    for copy in ws_copies:
        copy.wait_recv()
    for part in range(2):
        far[part] = term([gab[0, part], gab[1, part]], 0)

    some = scl.at[pl.ds(1, nl - 1)]
    remote(some, some, scl_send, scl_recv, leaf=me_l).wait_recv()
    match = hot[...]
    grown = jnp.exp(scl[:, 0:1, :])
    count = seen[...]
    node_total = jnp.sum(match * grown, axis=0, keepdims=True)
    node_seen = jnp.sum(match * count, axis=0, keepdims=True)
    total = jnp.sum(match * node_total, axis=2, keepdims=True)
    total_seen = jnp.sum(match * node_seen, axis=2, keepdims=True)
    scales = (LOSS_SCALE / tokens) * (grown / total - count / total_seen)
    cw[...] = scales * scl[:, 1:2, :]
    outs.append(pltpu.make_async_copy(cw, cw_out, out_sem.at[1]))
    outs[1].start()
    scale = scales[0, :, 0:1]

    rs_copies = []

    def rs_send_rows(value, target):
        slot = len(rs_copies)
        rs_s[slot] = value.astype(BF16)
        copy = remote(
            rs_s.at[slot], rs_r.at[slot], rs_send.at[slot], rs_recv.at[slot], head=target
        )
        copy.start()
        rs_copies.append(copy)

    first, second = slice(0, half), slice(half, tokens)
    rs_send_rows(far[0, first] + scale * far[1, first], right)
    rs_send_rows(far[0, second] + scale * far[1, second], left)

    def send_keys(i):
        total = dk[0, i] + scale * dk[1, i]
        dks[pl.ds(i * per, per)] = total.astype(BF16).reshape(per, rows, width)
        for slot in range(i * per, (i + 1) * per):
            if slot == 0:
                dkr[0] = dks[0]
            else:
                send_rows(dks, dkr, dk_send, dk_recv, slot)

    for i in range(chunks // 2):
        send_keys(i)
    for side in range(2):
        for at in range(0, tokens, TILE):
            tile = slice(at, at + TILE)
            grad = gab[side, 0, tile].astype(F32) + scale * gab[side, 1, tile].astype(F32)
            gg[side, tile] = grad.astype(BF16)
    ps[0] = term(gg, 1)
    rs_send_rows(ps[0, second], right)
    ps[1] = term(gg, 2)
    rs_send_rows(ps[1, first], left)
    for i in range(chunks // 2, chunks):
        send_keys(i)
    rs_copies[0].wait_recv()
    rs_send_rows(ps[0, first] + rs_r[0].astype(F32), right)
    rs_copies[1].wait_recv()
    rs_send_rows(ps[1, second] + rs_r[1].astype(F32), left)
    ps[2] = term(gg, 3)

    some = dvr.at[pl.ds(1, nl - 1)]
    remote(some, some, dv_send, dv_recv, leaf=me_l).wait_recv()
    outs.append(pltpu.make_async_copy(dvr, dv_out, out_sem.at[2]))
    outs[2].start()
    remote(some, some, dk_send, dk_recv, leaf=me_l).wait_recv()
    outs.append(pltpu.make_async_copy(dkr, dk_out, out_sem.at[3]))
    outs[3].start()

    for slot in range(2, 6):
        rs_copies[slot].wait_recv()
    gh[first, :] = (ps[2, first] + rs_r[4].astype(F32) + rs_r[3].astype(F32)).astype(BF16)
    gh[second, :] = (ps[2, second] + rs_r[2].astype(F32) + rs_r[5].astype(F32)).astype(BF16)

    outs.append(pltpu.make_async_copy(gh, gh_out, out_sem.at[4]))
    outs[4].start()

    for copy in ag + ws_copies + gx_copies + rs_copies:
        copy.wait_send()
    for buffer, send, recv in (
        (par, par_send, par_recv),
        (kvs, kv_send, kv_recv.at[0]),
        (dvs, dv_send, dv_recv),
        (dks, dk_send, dk_recv),
        (sls, scl_send, scl_recv),
    ):
        some = buffer.at[pl.ds(0, nl - 1)]
        remote(some, some, send, recv, leaf=me_l).wait_send()
    some = sch.at[pl.ds(1, ng - 1)]
    remote(some, some, sch_send, sch_recv, head=me_g).wait_send()
    for out in outs:
        out.wait()


def collect_kernel(par, readout, cw, dk_in, dv_in, gh_in, gh, gk, gv, key_total, value_total, sums):
    nodes, rows, width = gk.shape
    key_total[...] = jnp.zeros_like(key_total)
    value_total[...] = jnp.zeros_like(value_total)
    sums[...] = jnp.zeros_like(sums)

    def add(s, c):
        node = par[s, 0, 0]
        key_total[node] += dk_in[s].astype(F32)
        value_total[node] += dv_in[s].astype(F32)
        sums[node] += cw[s]
        return c

    lax.fori_loop(0, dk_in.shape[0], add, 0, unroll=4)
    gk[...] = key_total[...].astype(BF16)
    shape = (1, rows, 128)
    keep = lax.broadcasted_iota(jnp.int32, shape, 2) % rows == lax.broadcasted_iota(
        jnp.int32, shape, 1
    )
    left = jnp.where(keep, sums[...], 0.0).reshape(nodes * rows, 128)
    high = left.astype(BF16)
    rest = (left - high.astype(F32)).astype(BF16)
    right = jnp.concatenate(
        [
            jnp.broadcast_to(
                readout[h * width : (h + 1) * width].astype(F32).reshape(1, width), (rows, width)
            )
            for h in range(128 // rows)
        ],
        0,
    ).astype(BF16)
    extra = dot_nn(high, right) + dot_nn(rest, right)
    gv[...] = (value_total[...] + extra.reshape(nodes, rows, width)).astype(BF16)
    gh[...] = gh_in[...]


def per_device(
    ny,
    hidden_states,
    upper_gradient,
    w_query,
    key_projection,
    value_projection,
    query_gain,
    key_norm_gain,
    readout,
    cached_prefix_keys,
    cached_prefix_values,
    prefix_lengths,
    parents,
    visits,
):
    nl, ng = lax.axis_size("leaf"), lax.axis_size("head")
    nodes, rows, width = cached_prefix_keys.shape
    tokens, feats = hidden_states.shape
    model = w_query.shape[0]
    blocks = nl // (2 * ny) + 1
    span = max(2 * ny * rows, tokens)
    half = tokens // 2
    cols = (GROUP + 2) * width
    inverse = np.asarray(
        ROPE_BASE ** (-2.0 * (np.arange(width) % (width // 2)) / width), np.float32
    ).reshape(1, width)
    smem = pl.BlockSpec(memory_space=pltpu.SMEM)
    vmem = pl.BlockSpec(memory_space=pltpu.VMEM)
    anywhere = pl.BlockSpec(memory_space=pl.ANY)
    hbm = pl.BlockSpec(memory_space=pltpu.HBM)
    dma = pltpu.SemaphoreType.DMA
    rows_of_all = pltpu.VMEM((nl, rows, width), BF16)
    scratch = [
        pltpu.VMEM((1, width), F32),
        pltpu.VMEM((1, width), F32),
        pltpu.VMEM((1, width), F32),
        pltpu.VMEM((GROUP * width,), BF16),
        pltpu.VMEM((model, cols), BF16),
        pltpu.VMEM((4, feats, cols), BF16),
        pltpu.VMEM((ng, tokens, feats), BF16),
        pltpu.VMEM((nodes, rows, width), BF16),
        pltpu.VMEM((nodes, rows, width), BF16),
        pltpu.VMEM((tokens, GROUP * width), BF16),
        pltpu.VMEM((GROUP, tokens, 2 * width), BF16),
        pltpu.VMEM((1,), jnp.int32),
        pltpu.VMEM((1,), jnp.int32),
        pltpu.VMEM((nl, 1, 128), jnp.int32),
        pltpu.VMEM((nl, 1, 128), jnp.int32),
        pltpu.VMEM((nl, 1, 128), F32),
        pltpu.VMEM((tokens, feats), BF16),
        pltpu.VMEM((nl, 1, 128), F32),
        pltpu.VMEM((nl, 1, 128), F32),
        pltpu.VMEM((nl, 2, rows, width), BF16),
        pltpu.VMEM((nl, 2, rows, width), BF16),
        pltpu.VMEM((tokens, cols), F32),
        pltpu.VMEM((tokens, width), F32),
        pltpu.VMEM((tokens, width), F32),
        pltpu.VMEM((GROUP, tokens, width), BF16),
        pltpu.VMEM((2, tokens, width), BF16),
        pltpu.VMEM((blocks, GROUP, span, tokens), F32),
        pltpu.VMEM((blocks, GROUP, span, tokens), F32),
        pltpu.VMEM((blocks, span, 16), F32),
        pltpu.VMEM((GROUP, tokens), F32),
        pltpu.VMEM((GROUP, tokens), F32),
        pltpu.VMEM((GROUP, tokens), F32),
        pltpu.VMEM((blocks, GROUP, tokens), F32),
        pltpu.VMEM((blocks, span, 2 * width), F32),
        pltpu.VMEM((2, blocks, GROUP, span, tokens), BF16),
        pltpu.VMEM((2, blocks - 1, 2 * ny * rows, width), F32),
        pltpu.VMEM((ng, 1, 128), F32),
        pltpu.VMEM((nl, 2, 128), F32),
        pltpu.VMEM((nl, 2, 128), F32),
        rows_of_all,
        rows_of_all,
        rows_of_all,
        rows_of_all,
        pltpu.VMEM((GROUP + 2, 2, tokens, width), BF16),
        pltpu.VMEM((GROUP + 2, 2, tokens, width), BF16),
        pltpu.VMEM((2, 2, tokens, cols), BF16),
        pltpu.VMEM((2, tokens, cols), BF16),
        pltpu.VMEM((2, tokens, feats), F32),
        pltpu.VMEM((3, tokens, feats), F32),
        pltpu.VMEM((6, half, feats), BF16),
        pltpu.VMEM((6, half, feats), BF16),
        dma((13,)),
        dma,
        dma((blocks,)),
        dma((5,)),
        dma,
        dma((blocks - 1,)),
        dma((14,)),
        dma((ng, 2)),
        dma((4,)),
        dma((4,)),
        dma,
        dma,
        dma,
        dma,
        dma,
        dma,
        dma,
        dma,
        dma((GROUP + 2,)),
        dma((GROUP + 2,)),
        dma((6,)),
        dma((6,)),
    ]
    table = jax.ShapeDtypeStruct((nodes, rows, width), BF16)
    per_slot = jax.ShapeDtypeStruct((nl, rows, width), BF16)
    grad_hidden = jax.ShapeDtypeStruct((tokens, feats), BF16)
    gh, dk, dv, cw, par = pl.pallas_call(
        functools.partial(main_kernel, ny),
        out_shape=(
            grad_hidden,
            per_slot,
            per_slot,
            jax.ShapeDtypeStruct((nl, 1, 128), F32),
            jax.ShapeDtypeStruct((nl, 1, 128), jnp.int32),
        ),
        in_specs=[hbm, hbm, smem, hbm] + [anywhere] * 5 + [hbm] * 3 + [anywhere] * 2,
        out_specs=(anywhere,) * 5,
        scratch_shapes=scratch,
        compiler_params=pltpu.CompilerParams(
            collective_id=0, has_side_effects=True, vmem_limit_bytes=58 * 1024 * 1024
        ),
    )(
        parents,
        visits,
        prefix_lengths,
        jnp.asarray(inverse),
        hidden_states,
        upper_gradient,
        w_query,
        key_projection,
        value_projection,
        query_gain.reshape(1, width),
        key_norm_gain.reshape(1, width),
        readout,
        cached_prefix_keys,
        cached_prefix_values,
    )
    return pl.pallas_call(
        collect_kernel,
        out_shape=(grad_hidden, table, table),
        in_specs=[smem] + [vmem] * 5,
        out_specs=(vmem,) * 3,
        scratch_shapes=[
            pltpu.VMEM((nodes, rows, width), F32),
            pltpu.VMEM((nodes, rows, width), F32),
            pltpu.VMEM((nodes, 1, 128), F32),
        ],
        compiler_params=pltpu.CompilerParams(vmem_limit_bytes=58 * 1024 * 1024),
    )(par, readout, cw, dk, dv, gh)


def solution(mesh):
    in_specs = (
        P("leaf", "head"),
        P("leaf", "head"),
        P(None, "head"),
        P(None, "head"),
        P(None, "head"),
        P(),
        P(),
        P("head"),
        P(None, "leaf", "head"),
        P(None, "leaf", "head"),
        P(),
        P("leaf"),
        P("leaf"),
    )
    out_specs = (P("leaf", "head"), P(None, "leaf", "head"), P(None, "leaf", "head"))
    ny = 4 if mesh.shape["leaf"] % 4 == 0 else 1
    return jax.shard_map(
        functools.partial(per_device, ny),
        mesh=mesh,
        in_specs=in_specs,
        out_specs=out_specs,
        check_vma=False,
    )
```

```python
import functools

import jax
import jax.numpy as jnp
import numpy as np
from jax import lax
from jax.experimental import pallas as pl
from jax.experimental.pallas import tpu as pltpu
from jax.sharding import PartitionSpec as P

HEAD_SIZE = 128
GROUP = 4
EPS = 1e-06
ROPE_BASE = 1000000.0
LOSS_SCALE = 8192.0
SCALE = HEAD_SIZE ** (-0.5)
TILE = 64
BF16 = jnp.bfloat16
F32 = jnp.float32


def dot_nn(a, b):
    return lax.dot_general(a, b, (((1,), (0,)), ((), ())), preferred_element_type=F32)


def dot_nt(a, b):
    return lax.dot_general(a, b, (((1,), (1,)), ((), ())), preferred_element_type=F32)


def dot_tn(a, b):
    return lax.dot_general(a, b, (((0,), (0,)), ((), ())), preferred_element_type=F32)


def slot_offsets(nz, ny):
    order = [0]
    for step in range(1, nz // 2 + 1):
        order.append(step)
        if len(order) < nz:
            order.append(-step)
    return [(dz, dy) for dz in order for dy in range(ny)]


def main_kernel(
    ny,
    parents,
    visits,
    lengths,
    freq_in,
    hid,
    upper,
    wq,
    wk,
    wv,
    qgain_in,
    kgain_in,
    readout_in,
    ck,
    cv,
    gh_out,
    dk_out,
    gv_out,
    par_out,
    freq,
    qgain,
    kgain,
    readout,
    w,
    wsib,
    hf,
    cks,
    cvs,
    up,
    ue,
    own_parent,
    own_visits,
    par,
    par_slots,
    cw,
    gh,
    hot,
    seen,
    kvs,
    kvf,
    acc,
    cosb,
    sinb,
    q,
    own,
    e,
    uv,
    rv,
    lsum,
    asum,
    bsum,
    tops,
    dv,
    gl,
    dk,
    sch,
    sls,
    scl,
    dvs,
    dvr,
    dks,
    dkr,
    gvs,
    gx,
    gxr,
    gab,
    gg,
    far,
    ps,
    rs_s,
    rs_r,
    in_sem,
    par_send,
    par_recv,
    out_sem,
    kv_send,
    kv_recv,
    ag_send,
    ag_recv,
    ws_send,
    ws_recv,
    sch_send,
    sch_recv,
    scl_send,
    scl_recv,
    dv_send,
    dv_recv,
    dk_send,
    dk_recv,
    gx_send,
    gx_recv,
    rs_send,
    rs_recv,
):
    me_l = lax.axis_index("leaf")
    me_g = lax.axis_index("head")
    nl = lax.axis_size("leaf")
    ng = lax.axis_size("head")
    nz = nl // ny
    nx = ng // 2
    z, y = me_l // ny, me_l % ny
    x, core = me_g // 2, me_g % 2
    nodes, rows, width = ck.shape
    tokens, feats = hid.shape
    half = tokens // 2
    offsets = slot_offsets(nz, ny)
    place = {(dz % nz, dy): slot for slot, (dz, dy) in enumerate(offsets)}
    mirror = [place[(-dz % nz, -dy % ny)] for dz, dy in offsets]
    per = 2 * ny
    chunks = nl // per

    def chip(dx, other=False):
        side = 1 - core if other else core
        return ((x + dx + nx) % nx) * 2 + side

    def leaf_of(slot):
        dz, dy = offsets[slot]
        return ((z + dz + nz) % nz) * ny + (y + dy) % ny

    def remote(src, dst, send, recv, **target):
        return pltpu.make_async_remote_copy(
            src_ref=src,
            dst_ref=dst,
            send_sem=send,
            recv_sem=recv,
            device_id=target,
            device_id_type=pl.DeviceIdType.MESH,
        )

    barrier = pltpu.get_barrier_semaphore()
    for slot in reversed(range(1, nl)):
        pl.semaphore_signal(
            barrier, inc=1, device_id={"leaf": leaf_of(slot)}, device_id_type=pl.DeviceIdType.MESH
        )
    for o in range(1, ng):
        pl.semaphore_signal(
            barrier, inc=1, device_id={"head": (me_g + o) % ng}, device_id_type=pl.DeviceIdType.MESH
        )
    loads = [
        pltpu.make_async_copy(hid, hf.at[me_g], in_sem.at[0]),
        pltpu.make_async_copy(ck, cks, in_sem.at[1]),
        pltpu.make_async_copy(cv, cvs, in_sem.at[2]),
        pltpu.make_async_copy(wq, w.at[:, pl.ds(0, GROUP * width)], in_sem.at[3]),
        pltpu.make_async_copy(wk, w.at[:, pl.ds(GROUP * width, width)], in_sem.at[4]),
        pltpu.make_async_copy(wv, w.at[:, pl.ds((GROUP + 1) * width, width)], in_sem.at[5]),
        pltpu.make_async_copy(upper, up, in_sem.at[6]),
    ]
    small_loads = [
        pltpu.make_async_copy(freq_in, freq, in_sem.at[9]),
        pltpu.make_async_copy(qgain_in, qgain, in_sem.at[10]),
        pltpu.make_async_copy(kgain_in, kgain, in_sem.at[11]),
        pltpu.make_async_copy(readout_in, readout, in_sem.at[12]),
    ]
    first_loads = [
        pltpu.make_async_copy(parents, own_parent, in_sem.at[7]),
        pltpu.make_async_copy(visits, own_visits, in_sem.at[8]),
    ]
    for load in first_loads + loads[:3]:
        load.start()

    lane = lax.broadcasted_iota(jnp.int32, (1, 128), 1)
    for load in first_loads:
        load.wait()
    parent = own_parent[0]
    par[pl.ds(me_l, 1)] = jnp.where(lane == 0, parent, own_visits[0]).reshape(1, 1, 128)
    pl.semaphore_wait(barrier, nl - 1 + ng - 1)

    planes = [0] + [abs(dz) for dz, _ in offsets[ny::ny]]
    for slot in range(1, nl):
        remote(
            par.at[me_l],
            par.at[me_l],
            par_send,
            par_recv.at[planes[slot // ny]],
            leaf=leaf_of(slot),
        ).start()

    loads[0].wait()

    def ag_copy(sem, block, part, target):
        rows_at = hf.at[block, pl.ds(part * half, half)]
        return remote(rows_at, rows_at, ag_send.at[sem], ag_recv.at[block, part], head=target)

    def ag_wait(block, part):
        rows_at = hf.at[block, pl.ds(part * half, half)]
        remote(rows_at, rows_at, ag_send.at[0], ag_recv.at[block, part], head=me_g).wait_recv()

    right, left, sibling = chip(1), chip(-1), chip(0, True)
    ag = [
        ag_copy(0, me_g, 0, right),
        ag_copy(1, me_g, 1, left),
        ag_copy(2, me_g, 1, right),
        ag_copy(3, me_g, 0, left),
        ag_copy(4, me_g, 0, sibling),
        ag_copy(5, me_g, 1, sibling),
    ]
    for copy in ag:
        copy.start()
    for load in loads[3:] + small_loads:
        load.start()

    loads[1].wait()
    loads[2].wait()
    for plane in range(nz // 2 + 1):
        members = [slot for slot in range(nl) if planes[slot // ny] == plane]
        some = par.at[pl.ds(0, len([slot for slot in members if slot > 0]))]
        remote(some, some, par_send, par_recv.at[plane], leaf=me_l).wait_recv()
        for slot in members:
            dest = leaf_of(mirror[slot])
            node = par[dest, 0, 0]
            if slot == 0:
                kvf[0, 0] = cks[node]
                kvf[0, 1] = cvs[node]
            else:
                kvs[slot, 0] = cks[node]
                kvs[slot, 1] = cvs[node]
                remote(
                    kvs.at[slot], kvf.at[slot], kv_send, kv_recv.at[slot // per], leaf=dest
                ).start()

    def pass_on(*copies):
        for copy in copies:
            copy.start()
            ag.append(copy)

    ag_wait(left, 0)
    pass_on(ag_copy(6, left, 0, right), ag_copy(7, left, 0, sibling))
    ag_wait(right, 1)
    pass_on(ag_copy(8, right, 1, left), ag_copy(9, right, 1, sibling))

    for slot in range(nl):
        src = leaf_of(slot)
        par_row = jnp.full((1, 128), par[src, 0, 0], jnp.int32)
        par_slots[slot] = par_row
        hot[slot] = jnp.where((lane == par_row) & (lane < nodes), 1.0, 0.0)
        seen[slot] = jnp.full((1, 128), par[src, 0, 1], jnp.int32).astype(F32)
    outs = [pltpu.make_async_copy(par_slots, par_out, out_sem.at[0])]
    outs[0].start()

    for load in small_loads:
        load.wait()
    length = lengths[parent]
    position = (length + lax.broadcasted_iota(jnp.int32, (tokens, width), 0)).astype(F32)
    angle = position * freq[...]
    cosb[...] = jnp.cos(angle)
    low = lax.broadcasted_iota(jnp.int32, (tokens, width), 1) < width // 2
    sine = jnp.sin(angle)
    sinb[...] = jnp.where(low, -sine, sine)

    def rotate(value):
        return value * cosb[...] + pltpu.roll(value, width // 2, 1) * sinb[...]

    def rotate_back(value):
        return value * cosb[...] - pltpu.roll(value, width // 2, 1) * sinb[...]

    loads[6].wait()
    at_lane = lax.broadcasted_iota(jnp.int32, (tokens, width), 1)
    for h in range(GROUP):
        ue[h, :, 0:width] = up[:, h * width : (h + 1) * width]
        ue[h, :, width : 2 * width] = jnp.where(at_lane == h, 1.0, 0.0).astype(BF16)
    read = [readout[h * width : (h + 1) * width].astype(F32).reshape(1, width) for h in range(GROUP)]
    read_rows = jnp.concatenate(read + [jnp.zeros((16 - GROUP, width), F32)], 0).astype(BF16)

    for i in (3, 4, 5):
        loads[i].wait()

    def block_rows(block):
        return pl.ds(pl.multiple_of(block * feats, feats), feats)

    def project(block, first=False):
        part = dot_nn(hf[block], w[block_rows(block), :])
        if first:
            acc[...] = part
        else:
            acc[...] += part

    def keys_of(i, which=0):
        if i == chunks:
            return own[which]
        return kvf[pl.ds(i * per, per), which].reshape(per * rows, width)

    def wait_rows(i):
        skip = 1 if i == 0 else 0
        some = kvf.at[pl.ds(i * per + skip, per - skip)]
        remote(some, some, kv_send, kv_recv.at[i], leaf=me_l).wait_recv()

    def values_product(i):
        values = keys_of(i, 1)
        for h in range(GROUP):
            uv[i, h] = dot_nt(values, up[:, h * width : (h + 1) * width])
        rv[i] = dot_nt(values, read_rows)

    project(me_g, True)

    ag_wait(sibling, 0)
    ag_wait(sibling, 1)
    project(sibling)
    ag_wait(left, 1)
    ag_wait(right, 0)
    pass_on(ag_copy(10, left, 1, sibling), ag_copy(11, right, 0, sibling))
    project(left)
    project(right)

    def project_other(dx):
        block = chip(dx, True)
        ag_wait(block, 0)
        ag_wait(block, 1)
        project(block)

    project_other(-1)
    project_other(1)
    wait_rows(0)
    values_product(0)
    opposite = chip(2)
    ag_wait(opposite, 0)
    pass_on(ag_copy(12, opposite, 0, sibling))
    ag_wait(opposite, 1)
    pass_on(ag_copy(13, opposite, 1, sibling))
    project(opposite)
    project_other(2)

    hops = (2, 1, -1, 0)
    ws_copies = []
    for j, dx in enumerate(hops):
        copy = remote(
            w.at[block_rows(chip(dx, True))], wsib.at[j], ws_send.at[j], ws_recv.at[j], head=sibling
        )
        copy.start()
        ws_copies.append(copy)

    def norm_inverse(raw):
        return lax.rsqrt(jnp.mean(raw * raw, axis=-1, keepdims=True) + EPS)

    for h in range(GROUP + 1):
        raw = acc[:, h * width : (h + 1) * width]
        gain = qgain[...] if h < GROUP else kgain[...]
        turned = rotate(raw * norm_inverse(raw) * gain).astype(BF16)
        if h < GROUP:
            q[h] = turned
        else:
            own[0] = turned
    own[1] = acc[:, (GROUP + 1) * width :].astype(BF16)

    def forward(i, first):
        keys = keys_of(i)
        if i == chunks:
            shape = (tokens, tokens)
            mask = lax.broadcasted_iota(jnp.int32, shape, 0) <= lax.broadcasted_iota(
                jnp.int32, shape, 1
            )
        else:
            at = lax.broadcasted_iota(jnp.int32, (rows, tokens), 0)
            mask = (
                jnp.concatenate([at + leaf_of(i * per + b) * rows for b in range(per)], 0) < length
            )
        for h in range(GROUP):
            logits = jnp.where(mask, dot_nt(keys, q[h]) * SCALE, -1e30)
            top = jnp.max(logits, axis=0, keepdims=True)
            if not first:
                before = tops[i_last[0], h : h + 1, :]
                top = jnp.maximum(top, before)
            weight = jnp.exp(logits - top)
            total = jnp.sum(weight, axis=0, keepdims=True)
            a = jnp.sum(weight * rv[i][:, h : h + 1], axis=0, keepdims=True)
            if not first:
                fade = jnp.exp(before - top)
                total += lsum[h : h + 1, :] * fade
                a += asum[h : h + 1, :] * fade
            lsum[h : h + 1, :] = total
            asum[h : h + 1, :] = a
            tops[i, h : h + 1, :] = top
            e[i, h] = weight
        i_last[0] = i

    i_last = [None]
    values_product(chunks)
    forward(chunks, True)
    forward(0, False)
    for i in range(1, chunks):
        wait_rows(i)
        values_product(i)
        forward(i, False)

    score = jnp.zeros((1, 1), F32)
    for h in range(GROUP):
        inverse = 1.0 / lsum[h : h + 1, :]
        lsum[h : h + 1, :] = inverse
        a = asum[h : h + 1, :] * inverse
        asum[h : h + 1, :] = a
        score += jnp.sum(a, axis=1, keepdims=True)
    sch[0] = jnp.broadcast_to(score / tokens, (1, 128))
    for o in range(1, ng):
        remote(sch.at[0], sch.at[o], sch_send, sch_recv, head=(me_g + o) % ng).start()

    for h in range(GROUP):
        b = jnp.zeros((1, tokens), F32)
        for i in range(chunks + 1):
            factor = lsum[h : h + 1, :]
            if i != chunks - 1:
                factor *= jnp.exp(tops[i, h : h + 1, :] - tops[chunks - 1, h : h + 1, :])
            for at in range(0, keys_of(i).shape[0], TILE):
                tile = slice(at, at + TILE)
                prob = e[i, h, tile] * factor
                e[i, h, tile] = prob
                gl[0, i, h, tile] = prob.astype(BF16)
                b += jnp.sum(prob * uv[i, h, tile], axis=0, keepdims=True)
            term = dot_nn(gl[0, i, h], ue[h])
            if h == 0:
                dv[i] = term
            else:
                dv[i] += term
        bsum[h : h + 1, :] = b

    def send_rows(buffer, target, send, recv, slot):
        remote(buffer.at[slot], target.at[mirror[slot]], send, recv, leaf=leaf_of(slot)).start()

    def send_values(i):
        dvs[pl.ds(i * per, per)] = dv[i][:, :width].astype(BF16).reshape(per, rows, width)
        for slot in range(i * per, (i + 1) * per):
            if slot == 0:
                dvr[0] = dvs[0]
            else:
                send_rows(dvs, dvr, dv_send, dv_recv, slot)

    parts = 128 // rows
    group = lane // rows
    diagonal = lax.broadcasted_iota(jnp.int32, (8, 128), 0) == lax.broadcasted_iota(
        jnp.int32, (8, 128), 1
    ) // rows
    for i in range(chunks):
        sums = dv[i][:, width:].T[0:8]
        for j in range(per // parts):
            tile = sums[:, j * 128 : (j + 1) * 128]
            turns = []
            for k in range(parts):
                moved = tile if k == 0 else pltpu.roll(tile, rows * k, 1)
                turns.append(jnp.sum(jnp.where(diagonal, moved, 0.0), axis=0, keepdims=True))
            for b in range(parts):
                line = turns[(0 - b) % parts]
                for h in range(1, parts):
                    line = jnp.where(group == h, turns[(h - b) % parts], line)
                sls[i * per + j * parts + b, 1:2] = line

    def norm_back(raw, gain, grad):
        inverse = norm_inverse(raw)
        scaled = grad * gain
        mean = jnp.mean(raw * scaled, axis=-1, keepdims=True)
        return (inverse * scaled - raw * (inverse * inverse * inverse) * mean).astype(BF16)

    gx_copies = [
        remote(gx.at[j], gxr.at[j], gx_send.at[j], gx_recv.at[j], head=sibling)
        for j in range(GROUP + 2)
    ]

    def query_grads(h):
        back = [None, None]
        for i in range(chunks + 1):
            keys = keys_of(i)
            for at in range(0, keys.shape[0], TILE):
                tile = slice(at, at + TILE)
                prob = e[i, h, tile] * SCALE
                grad = prob * (uv[i, h, tile] - bsum[h : h + 1, :])
                gl[0, i, h, tile] = grad.astype(BF16)
                grad = prob * (rv[i, tile, h : h + 1] - asum[h : h + 1, :])
                gl[1, i, h, tile] = grad.astype(BF16)
            for part in range(2):
                term = dot_tn(keys, gl[part, i, h])
                back[part] = term if i == 0 else back[part] + term
        raw = acc[:, h * width : (h + 1) * width]
        for part in range(2):
            gx[h, part] = norm_back(raw, qgain[...], rotate_back(back[part].T))
        gx_copies[h].start()

    query_grads(0)
    query_grads(1)

    some = sch.at[pl.ds(1, ng - 1)]
    remote(some, some, sch_send, sch_recv, head=me_g).wait_recv()
    step_score = jnp.sum(sch[...], axis=0)
    for slot in range(nl):
        sls[slot, 0:1] = step_score
    scl[0] = sls[0]
    for slot in reversed(range(1, nl)):
        send_rows(sls, scl, scl_send, scl_recv, slot)
    for i in range(1):
        send_values(i)
    query_grads(2)
    for i in range(1,4):
        send_values(i)
    query_grads(3)

    read_value = None
    for h in range(GROUP):
        term = dv[chunks][:, width + h : width + h + 1] * read[h]
        read_value = term if read_value is None else read_value + term
    gx[GROUP + 1, 0] = dv[chunks][:, :width].astype(BF16)
    gx[GROUP + 1, 1] = read_value.astype(BF16)
    gx_copies[GROUP + 1].start()
    for part in range(2):
        back = None
        for h in range(GROUP):
            term = dot_nn(gl[part, chunks, h], q[h])
            back = term if back is None else back + term
        cols = slice(GROUP * width, (GROUP + 1) * width)
        gx[GROUP, part] = norm_back(acc[:, cols], kgain[...], rotate_back(back))
    gx_copies[GROUP].start()

    for i in range(chunks):
        for part in range(2):
            total = None
            for h in range(GROUP):
                product = dot_nn(gl[part, i, h], q[h])
                total = product if total is None else total + product
            dk[part, i] = total
    for j in range(GROUP + 2):
        cols = slice(j * width, (j + 1) * width)
        gx_copies[j].wait_recv()
        for part in range(2):
            gab[0, part, :, cols] = gx[j, part]
            gab[1, part, :, cols] = gxr[j, part]

    def term(left, j):
        return dot_nt(left[0], w[block_rows(chip(hops[j])), :]) + dot_nt(left[1], wsib[j])

    for copy in ws_copies:
        copy.wait_recv()
    for part in range(2):
        far[part] = term([gab[0, part], gab[1, part]], 0)

    some = scl.at[pl.ds(1, nl - 1)]
    remote(some, some, scl_send, scl_recv, leaf=me_l).wait_recv()
    match = hot[...]
    grown = jnp.exp(scl[:, 0:1, :])
    count = seen[...]
    node_total = jnp.sum(match * grown, axis=0, keepdims=True)
    node_seen = jnp.sum(match * count, axis=0, keepdims=True)
    total = jnp.sum(match * node_total, axis=2, keepdims=True)
    total_seen = jnp.sum(match * node_seen, axis=2, keepdims=True)
    scales = (LOSS_SCALE / tokens) * (grown / total - count / total_seen)
    cw[...] = scales * scl[:, 1:2, :]
    scale = scales[0, :, 0:1]

    rs_copies = []

    def rs_send_rows(value, target):
        slot = len(rs_copies)
        rs_s[slot] = value.astype(BF16)
        copy = remote(
            rs_s.at[slot], rs_r.at[slot], rs_send.at[slot], rs_recv.at[slot], head=target
        )
        copy.start()
        rs_copies.append(copy)

    first, second = slice(0, half), slice(half, tokens)
    rs_send_rows(far[0, first] + scale * far[1, first], right)
    rs_send_rows(far[0, second] + scale * far[1, second], left)

    def send_keys(i):
        total = dk[0, i] + scale * dk[1, i]
        dks[pl.ds(i * per, per)] = total.astype(BF16).reshape(per, rows, width)
        for slot in range(i * per, (i + 1) * per):
            if slot == 0:
                dkr[0] = dks[0]
            else:
                send_rows(dks, dkr, dk_send, dk_recv, slot)

    for i in range(chunks // 2):
        send_keys(i)
    for side in range(2):
        for at in range(0, tokens, TILE):
            tile = slice(at, at + TILE)
            grad = gab[side, 0, tile].astype(F32) + scale * gab[side, 1, tile].astype(F32)
            gg[side, tile] = grad.astype(BF16)
    ps[0] = term(gg, 1)
    rs_send_rows(ps[0, second], right)
    ps[1] = term(gg, 2)
    rs_send_rows(ps[1, first], left)
    for i in range(chunks // 2, chunks):
        send_keys(i)
    rs_copies[0].wait_recv()
    rs_send_rows(ps[0, first] + rs_r[0].astype(F32), right)
    rs_copies[1].wait_recv()
    rs_send_rows(ps[1, second] + rs_r[1].astype(F32), left)
    ps[2] = term(gg, 3)

    some = dvr.at[pl.ds(1, nl - 1)]
    remote(some, some, dv_send, dv_recv, leaf=me_l).wait_recv()
    shape = (nodes * rows, 128)
    at_node = lax.broadcasted_iota(jnp.int32, shape, 0) // rows
    same_row = lax.broadcasted_iota(jnp.int32, shape, 0) % rows == (
        lax.broadcasted_iota(jnp.int32, shape, 1) % rows
    )
    scaled = cw[...].reshape(nl, 128)
    picked = hot[...].reshape(nl, 128).astype(BF16)
    high = scaled.astype(BF16)
    rest = (scaled - high.astype(F32)).astype(BF16)
    sums = (dot_tn(picked, high) + dot_tn(picked, rest))[:nodes]
    spread = jnp.broadcast_to(sums[:, None, :], (nodes, rows, 128)).reshape(shape)
    spread = jnp.where(same_row, spread, 0.0)
    high = spread.astype(BF16)
    rest = (spread - high.astype(F32)).astype(BF16)
    lines = jnp.concatenate(
        [jnp.broadcast_to(read[h], (rows, width)) for h in range(GROUP)], 0
    ).astype(BF16)
    total_values = dot_nn(high, lines) + dot_nn(rest, lines)
    for k in range(nl // parts):
        line = par_slots[k * parts]
        for b in range(1, parts):
            line = jnp.where(group == b, par_slots[k * parts + b], line)
        pick = jnp.where((at_node == line) & same_row, 1.0, 0.0).astype(BF16)
        total_values += dot_nn(pick, dvr[k * parts : (k + 1) * parts].reshape(128, width))
    gvs[...] = total_values.astype(BF16).reshape(nodes, rows, width)
    outs.append(pltpu.make_async_copy(gvs, gv_out, out_sem.at[2]))
    outs[1].start()
    remote(some, some, dk_send, dk_recv, leaf=me_l).wait_recv()
    outs.append(pltpu.make_async_copy(dkr, dk_out, out_sem.at[3]))
    outs[2].start()

    for slot in range(2, 6):
        rs_copies[slot].wait_recv()
    gh[first, :] = (ps[2, first] + rs_r[4].astype(F32) + rs_r[3].astype(F32)).astype(BF16)
    gh[second, :] = (ps[2, second] + rs_r[2].astype(F32) + rs_r[5].astype(F32)).astype(BF16)

    outs.append(pltpu.make_async_copy(gh, gh_out, out_sem.at[4]))
    outs[3].start()

    for copy in ag + ws_copies + gx_copies + rs_copies:
        copy.wait_send()
    for buffer, send, recv in (
        (par, par_send, par_recv),
        (kvs, kv_send, kv_recv.at[0]),
        (dvs, dv_send, dv_recv),
        (dks, dk_send, dk_recv),
        (sls, scl_send, scl_recv),
    ):
        some = buffer.at[pl.ds(0, nl - 1)]
        remote(some, some, send, recv, leaf=me_l).wait_send()
    some = sch.at[pl.ds(1, ng - 1)]
    remote(some, some, sch_send, sch_recv, head=me_g).wait_send()
    for out in outs:
        out.wait()


def collect_kernel(par, dk_in, gv_in, gh_in, gh, gk, gv, total):
    total[...] = jnp.zeros_like(total)

    def add(s, c):
        total[par[s, 0, 0]] += dk_in[s].astype(F32)
        return c

    lax.fori_loop(0, dk_in.shape[0], add, 0, unroll=4)
    gk[...] = total[...].astype(BF16)
    gv[...] = gv_in[...]
    gh[...] = gh_in[...]


def per_device(
    ny,
    hidden_states,
    upper_gradient,
    w_query,
    key_projection,
    value_projection,
    query_gain,
    key_norm_gain,
    readout,
    cached_prefix_keys,
    cached_prefix_values,
    prefix_lengths,
    parents,
    visits,
):
    nl, ng = lax.axis_size("leaf"), lax.axis_size("head")
    nodes, rows, width = cached_prefix_keys.shape
    tokens, feats = hidden_states.shape
    model = w_query.shape[0]
    blocks = nl // (2 * ny) + 1
    span = max(2 * ny * rows, tokens)
    half = tokens // 2
    cols = (GROUP + 2) * width
    inverse = np.asarray(
        ROPE_BASE ** (-2.0 * (np.arange(width) % (width // 2)) / width), np.float32
    ).reshape(1, width)
    smem = pl.BlockSpec(memory_space=pltpu.SMEM)
    vmem = pl.BlockSpec(memory_space=pltpu.VMEM)
    anywhere = pl.BlockSpec(memory_space=pl.ANY)
    hbm = pl.BlockSpec(memory_space=pltpu.HBM)
    dma = pltpu.SemaphoreType.DMA
    rows_of_all = pltpu.VMEM((nl, rows, width), BF16)
    scratch = [
        pltpu.VMEM((1, width), F32),
        pltpu.VMEM((1, width), F32),
        pltpu.VMEM((1, width), F32),
        pltpu.VMEM((GROUP * width,), BF16),
        pltpu.VMEM((model, cols), BF16),
        pltpu.VMEM((4, feats, cols), BF16),
        pltpu.VMEM((ng, tokens, feats), BF16),
        pltpu.VMEM((nodes, rows, width), BF16),
        pltpu.VMEM((nodes, rows, width), BF16),
        pltpu.VMEM((tokens, GROUP * width), BF16),
        pltpu.VMEM((GROUP, tokens, 2 * width), BF16),
        pltpu.VMEM((1,), jnp.int32),
        pltpu.VMEM((1,), jnp.int32),
        pltpu.VMEM((nl, 1, 128), jnp.int32),
        pltpu.VMEM((nl, 1, 128), jnp.int32),
        pltpu.VMEM((nl, 1, 128), F32),
        pltpu.VMEM((tokens, feats), BF16),
        pltpu.VMEM((nl, 1, 128), F32),
        pltpu.VMEM((nl, 1, 128), F32),
        pltpu.VMEM((nl, 2, rows, width), BF16),
        pltpu.VMEM((nl, 2, rows, width), BF16),
        pltpu.VMEM((tokens, cols), F32),
        pltpu.VMEM((tokens, width), F32),
        pltpu.VMEM((tokens, width), F32),
        pltpu.VMEM((GROUP, tokens, width), BF16),
        pltpu.VMEM((2, tokens, width), BF16),
        pltpu.VMEM((blocks, GROUP, span, tokens), F32),
        pltpu.VMEM((blocks, GROUP, span, tokens), F32),
        pltpu.VMEM((blocks, span, 16), F32),
        pltpu.VMEM((GROUP, tokens), F32),
        pltpu.VMEM((GROUP, tokens), F32),
        pltpu.VMEM((GROUP, tokens), F32),
        pltpu.VMEM((blocks, GROUP, tokens), F32),
        pltpu.VMEM((blocks, span, 2 * width), F32),
        pltpu.VMEM((2, blocks, GROUP, span, tokens), BF16),
        pltpu.VMEM((2, blocks - 1, 2 * ny * rows, width), F32),
        pltpu.VMEM((ng, 1, 128), F32),
        pltpu.VMEM((nl, 2, 128), F32),
        pltpu.VMEM((nl, 2, 128), F32),
        rows_of_all,
        rows_of_all,
        rows_of_all,
        rows_of_all,
        pltpu.VMEM((nodes, rows, width), BF16),
        pltpu.VMEM((GROUP + 2, 2, tokens, width), BF16),
        pltpu.VMEM((GROUP + 2, 2, tokens, width), BF16),
        pltpu.VMEM((2, 2, tokens, cols), BF16),
        pltpu.VMEM((2, tokens, cols), BF16),
        pltpu.VMEM((2, tokens, feats), F32),
        pltpu.VMEM((3, tokens, feats), F32),
        pltpu.VMEM((6, half, feats), BF16),
        pltpu.VMEM((6, half, feats), BF16),
        dma((13,)),
        dma,
        dma((blocks,)),
        dma((5,)),
        dma,
        dma((blocks - 1,)),
        dma((14,)),
        dma((ng, 2)),
        dma((4,)),
        dma((4,)),
        dma,
        dma,
        dma,
        dma,
        dma,
        dma,
        dma,
        dma,
        dma((GROUP + 2,)),
        dma((GROUP + 2,)),
        dma((6,)),
        dma((6,)),
    ]
    table = jax.ShapeDtypeStruct((nodes, rows, width), BF16)
    per_slot = jax.ShapeDtypeStruct((nl, rows, width), BF16)
    grad_hidden = jax.ShapeDtypeStruct((tokens, feats), BF16)
    gh, dk, gv, par = pl.pallas_call(
        functools.partial(main_kernel, ny),
        out_shape=(
            grad_hidden,
            per_slot,
            table,
            jax.ShapeDtypeStruct((nl, 1, 128), jnp.int32),
        ),
        in_specs=[hbm, hbm, smem, hbm] + [anywhere] * 5 + [hbm] * 3 + [anywhere] * 2,
        out_specs=(anywhere,) * 4,
        scratch_shapes=scratch,
        compiler_params=pltpu.CompilerParams(
            collective_id=0, has_side_effects=True, vmem_limit_bytes=58 * 1024 * 1024
        ),
    )(
        parents,
        visits,
        prefix_lengths,
        jnp.asarray(inverse),
        hidden_states,
        upper_gradient,
        w_query,
        key_projection,
        value_projection,
        query_gain.reshape(1, width),
        key_norm_gain.reshape(1, width),
        readout,
        cached_prefix_keys,
        cached_prefix_values,
    )
    return pl.pallas_call(
        collect_kernel,
        out_shape=(grad_hidden, table, table),
        in_specs=[smem] + [vmem] * 3,
        out_specs=(vmem,) * 3,
        scratch_shapes=[pltpu.VMEM((nodes, rows, width), F32)],
        compiler_params=pltpu.CompilerParams(vmem_limit_bytes=58 * 1024 * 1024),
    )(par, dk, gv, gh)


def solution(mesh):
    in_specs = (
        P("leaf", "head"),
        P("leaf", "head"),
        P(None, "head"),
        P(None, "head"),
        P(None, "head"),
        P(),
        P(),
        P("head"),
        P(None, "leaf", "head"),
        P(None, "leaf", "head"),
        P(),
        P("leaf"),
        P("leaf"),
    )
    out_specs = (P("leaf", "head"), P(None, "leaf", "head"), P(None, "leaf", "head"))
    ny = 4 if mesh.shape["leaf"] % 4 == 0 else 1
    return jax.shard_map(
        functools.partial(per_device, ny),
        mesh=mesh,
        in_specs=in_specs,
        out_specs=out_specs,
        check_vma=False,
    )
```
